512 devices in a mesh: req: 8 (over z), cand: 32 (over y, x), user: 2 (over core).
Axes of the slice: x: 4, y: 8, z: 8, core: 2. Of those that a mesh axis runs over, the one named last changes fastest.
Arguments:
- table: bfloat16 [262144, 512], P(('req', 'cand')), may hold values from -6 to 6
- hot_table: bfloat16 [256, 512], replicated, may hold values from -6 to 6
- hot_ids: int32 [256], replicated, may hold values from 0 to 262143, as said below
- hist_ids: int32 [256, 1024], P(('req', 'cand'), 'user'), may hold values from 0 to 262143, as said below
- cand_ids: int32 [256, 1024], P(('req', 'cand'), 'user'), may hold values from 0 to 262143, as said below
- w_in: bfloat16 [1, 512, 2048], replicated, may hold values from -0.25 to 0.25
- w_out: bfloat16 [1, 512, 512], replicated, may hold values from -0.25 to 0.25
- in_gain: float32 [1, 512], replicated, may hold values from 0.25 to 1.75
- attn_gain: float32 [1, 512], replicated, may hold values from 0.25 to 1.75
Outputs:
- hist_out: bfloat16 [256, 1024, 512], P(('req', 'cand'), 'user')
- cand_out: bfloat16 [256, 1024, 512], P(('req', 'cand'), 'user')
The draws below stay inside these ranges and needn't reach their ends.
Inputs may be any that keep to these rules, and one draw needn't show every extreme that they name: `hot_ids`: distinct row ids. `hist_ids`: the owner of row id g is g // 1024, the index along req and cand together with req slowest. Of the 512 items of one device, those not in hot_ids have at most 4 items with any one owner, and one owner has exactly 4 of every device's items. `cand_ids`: of the 512 candidates of one device, those not in hot_ids have at most 3 candidates with any one owner, and one owner has exactly 3 of every device's candidates.
All inputs are finite; a program needn't handle non-finite values.
Results may differ from the reference program's by a relative error of at most 0.0055.
Values may be sent and summed in bfloat16 or wider, within the bound.
No kernel may reach another device: no remote copies, remote signals or barrier semaphores. Data moves between devices by JAX's collectives and lax.ppermute only.
A program may use at most 64 MiB of HBM per device.

```python
import jax
import jax.numpy as jnp
from jax import lax

D = 512
HEADS = 4
LAYERS = 1
HIST_DEV = 512
CAND_DEV = 512
ROWS_OWN = 1024
HOT = 256
HISTORY = 1024
CANDIDATES = 1024
REQS = 256
OWNERS = 256
TABLE_ROWS = 262144
CAP_H = 4
CAP_C = 3


def busiest_owner(key):
    return jax.random.randint(jax.random.fold_in(key, 101), (), 0, OWNERS)


def hot_list(key):
    busiest = busiest_owner(key)
    chosen = jax.random.permutation(jax.random.fold_in(key, 202), (OWNERS - 1) * ROWS_OWN)[:HOT]
    owner_of = (busiest + 1 + chosen // ROWS_OWN) % OWNERS
    return (owner_of * ROWS_OWN + chosen % ROWS_OWN).astype(jnp.int32)


def lookup_ids(key, salt, per_block, capacity, block_count):
    busiest = busiest_owner(key)
    hot_rows = hot_list(key)
    levels = jax.random.randint(jax.random.fold_in(key, 303), (OWNERS,), 0, 4)
    base_key = jax.random.fold_in(key, salt)
    slot_total = OWNERS * capacity
    slot_owner = jnp.arange(slot_total) // capacity

    def one_block(block_index):
        block_keys = jax.random.split(jax.random.fold_in(base_key, block_index), 5)
        noise = jax.random.randint(block_keys[0], (slot_total,), 0, 65536)
        scores = (levels[slot_owner] * 65536 + noise) * slot_total + jnp.arange(slot_total)
        scores = jnp.where(slot_owner == busiest, -1 - jnp.arange(slot_total), scores)
        unused, picked = lax.top_k(scores, per_block - capacity)
        owners_here = jnp.concatenate([jnp.full((capacity,), busiest, jnp.int32), slot_owner[picked].astype(jnp.int32)])
        row_numbers = jax.random.randint(block_keys[1], (per_block,), 0, ROWS_OWN)
        cold_ids = owners_here * ROWS_OWN + row_numbers
        hot_pick = hot_rows[jax.random.randint(block_keys[2], (per_block,), 0, HOT)]
        hot_flag = (jax.random.randint(block_keys[3], (per_block,), 0, 8) < 2) & (jnp.arange(per_block) >= capacity)
        row_ids = jnp.where(hot_flag, hot_pick, cold_ids).astype(jnp.int32)
        return row_ids[jax.random.permutation(block_keys[4], per_block)]
    return jax.vmap(one_block)(jnp.arange(block_count))


def draw_hot_ids(key, part):
    return hot_list(key)


def draw_hist_ids(key, part):
    block_count = REQS * HISTORY // HIST_DEV
    return lookup_ids(key, 404, HIST_DEV, CAP_H, block_count).reshape(REQS, HISTORY)


def draw_cand_ids(key, part):
    block_count = REQS * CANDIDATES // CAND_DEV
    return lookup_ids(key, 505, CAND_DEV, CAP_C, block_count).reshape(REQS, CANDIDATES)


def steps_of(own_key, shape, pieces, low, high):
    def one(position, blocks):
        heights = jax.random.uniform(jax.random.fold_in(jax.random.fold_in(own_key, 6), position), (blocks,), jnp.float32, low / len(pieces), high / len(pieces))
        return jnp.repeat(jnp.exp(heights), shape[position] // blocks).reshape((-1,) + (1,) * (len(shape) - position - 1))

    factor_of = one(*pieces[0])
    for cut in pieces[1:]:
        factor_of = factor_of * one(*cut)
    return factor_of


def bell_draw(stream_key, extent, spread, limit, cuts=(), held_as=jnp.bfloat16):
    drawn = jax.random.normal(stream_key, extent, jnp.float32) * spread
    if len(cuts) > 0:
        drawn = steps_of(stream_key, extent, cuts, -0.22, 0.18) * drawn
    return jnp.clip(drawn, min=-limit, max=limit).astype(held_as)


def setup_inputs(seed: int = 0) -> dict:
    arg_keys = jax.random.split(jax.random.key(seed), 10)
    return {
        "table": bell_draw(arg_keys[0], (TABLE_ROWS, D), 1.0, 6.0, ((0, 256),)),
        "hot_table": bell_draw(arg_keys[1], (HOT, D), 1.0, 6.0),
        "hot_ids": draw_hot_ids(jax.random.fold_in(arg_keys[9], 71), 0),
        "hist_ids": draw_hist_ids(jax.random.fold_in(arg_keys[9], 71), 0),
        "cand_ids": draw_cand_ids(jax.random.fold_in(arg_keys[9], 71), 0),
        "w_in": bell_draw(arg_keys[5], (LAYERS, D, 4 * D), D ** -0.5, 0.25),
        "w_out": bell_draw(arg_keys[6], (LAYERS, D, D), D ** -0.5, 0.25),
        "in_gain": jnp.clip(1.0 + 0.15 * jax.random.normal(arg_keys[7], (LAYERS, D), jnp.float32), 0.25, 1.75),
        "attn_gain": jnp.clip(1.0 + 0.15 * jax.random.normal(arg_keys[8], (LAYERS, D), jnp.float32), 0.25, 1.75),
    }


def norm_rows(values, scale_gain):
    centre_mean = lax.optimization_barrier(jnp.mean(values, axis=-1, keepdims=True))
    centred = values - centre_mean
    variance = lax.optimization_barrier(jnp.mean(centred * centred, axis=-1, keepdims=True))
    return centred * lax.rsqrt(variance + 1e-05) * scale_gain

def lookup_rows(row_ids, table, hot_ids, hot_table):
    hot_hit = row_ids[:, None] == hot_ids[None, :]
    is_hot = jnp.any(hot_hit, axis=1)
    hot_rows = jnp.dot(hot_hit.astype(jnp.bfloat16), hot_table, preferred_element_type=jnp.float32).astype(jnp.bfloat16)
    cold_rows = jnp.take(table, row_ids, axis=0)
    return jnp.where(is_hot[:, None], hot_rows, cold_rows)

def mix_heads(queries, keys, values, keep_mask):
    feature_count = queries.shape[1]
    head_dim = feature_count // HEADS
    query_heads = queries.astype(jnp.float32).reshape(queries.shape[0], HEADS, head_dim)
    key_heads = keys.astype(jnp.float32).reshape(keys.shape[0], HEADS, head_dim)
    value_heads = values.astype(jnp.float32).reshape(values.shape[0], HEADS, head_dim)
    scores = jnp.einsum('qhd,khd->hqk', query_heads, key_heads) * (1.0 / head_dim ** 0.5)
    weights = jnp.where(keep_mask[None], jax.nn.silu(scores), 0.0).astype(jnp.bfloat16)
    mixed = jnp.einsum('hqk,khd->qhd', weights.astype(jnp.float32), value_heads)
    return mixed.reshape(queries.shape[0], feature_count)

def reference(table, hot_table, hot_ids, hist_ids, cand_ids, w_in, w_out, in_gain, attn_gain):
    feature_count = table.shape[1]

    def one_request(id_pair):
        hist_row_ids, cand_row_ids = id_pair
        hist_x = lookup_rows(hist_row_ids, table, hot_ids, hot_table)
        cand_x = lookup_rows(cand_row_ids, table, hot_ids, hot_table)
        positions = jnp.arange(hist_row_ids.shape[0])
        causal = positions[None, :] <= positions[:, None]
        every_key = jnp.ones((cand_row_ids.shape[0], hist_row_ids.shape[0]), dtype=bool)
        for layer_index in range(LAYERS):
            weights_in = w_in[layer_index]
            hist_in = norm_rows(hist_x.astype(jnp.float32), in_gain[layer_index]).astype(jnp.bfloat16)
            cand_in = norm_rows(cand_x.astype(jnp.float32), in_gain[layer_index]).astype(jnp.bfloat16)
            projected = jax.nn.silu(jnp.dot(hist_in, weights_in, preferred_element_type=jnp.float32))
            hist_u = projected[:, :feature_count]
            hist_v = projected[:, feature_count:2 * feature_count].astype(jnp.bfloat16)
            hist_q = projected[:, 2 * feature_count:3 * feature_count].astype(jnp.bfloat16)
            hist_k = projected[:, 3 * feature_count:].astype(jnp.bfloat16)
            cand_u = jax.nn.silu(jnp.dot(cand_in, weights_in[:, :feature_count], preferred_element_type=jnp.float32))
            cand_q = jax.nn.silu(jnp.dot(cand_in, weights_in[:, 2 * feature_count:3 * feature_count], preferred_element_type=jnp.float32)).astype(jnp.bfloat16)
            hist_mix = mix_heads(hist_q, hist_k, hist_v, causal)
            cand_mix = mix_heads(cand_q, hist_k, hist_v, every_key)
            hist_gated = (norm_rows(hist_mix, attn_gain[layer_index]) * hist_u).astype(jnp.bfloat16)
            cand_gated = (norm_rows(cand_mix, attn_gain[layer_index]) * cand_u).astype(jnp.bfloat16)
            hist_x = (hist_x.astype(jnp.float32) + jnp.dot(hist_gated, w_out[layer_index], preferred_element_type=jnp.float32)).astype(jnp.bfloat16)
            cand_x = (cand_x.astype(jnp.float32) + jnp.dot(cand_gated, w_out[layer_index], preferred_element_type=jnp.float32)).astype(jnp.bfloat16)
        return (hist_x, cand_x)
    hist_out, cand_out = lax.map(one_request, (hist_ids, cand_ids))
    return (hist_out, cand_out)
```

```python
import jax
import jax.numpy as jnp
from jax import lax
from jax.experimental import pallas as pl
from jax.experimental.pallas import tpu as pltpu
from jax.sharding import PartitionSpec as P

HEADS = 4
SLOTS = 4
LANES = 8
F32 = jnp.float32
BF16 = jnp.bfloat16
I32 = jnp.int32
VMEM_BYTES = 32 * 1024 * 1024


def iota(shape, dim):
    return lax.broadcasted_iota(I32, shape, dim)


def dot(a, b):
    return jnp.dot(a, b, preferred_element_type=F32)


def dot_nt(a, b):
    return lax.dot_general(a, b, (((1,), (1,)), ((), ())), preferred_element_type=F32)


def to_column(row):
    n = row.shape[1]
    diag = iota((n, n), 0) == iota((n, n), 1)
    return jnp.sum(jnp.where(diag, row, 0.0), axis=1, keepdims=True)


def silu(v):
    half = 0.5 * v
    return half + half * jnp.tanh(half)


def norm(z, gain):
    centred = z - jnp.mean(z, axis=1, keepdims=True)
    variance = jnp.mean(centred * centred, axis=1, keepdims=True)
    return centred * lax.rsqrt(variance + 1e-05) * gain


def ask_kernel(hist_ids, cand_ids, hot_ids, asked, picks, *, owners, shift):
    hot_count = hot_ids.shape[1]
    hot_column = to_column(hot_ids[...].astype(F32))
    total = jnp.zeros((owners, LANES), F32)
    for side, (ids_ref, first) in enumerate(((hist_ids, 0), (cand_ids, SLOTS))):
        ids = ids_ref[...]
        n = ids.shape[1]
        hit = hot_column == ids.astype(F32)
        is_hot = jnp.max(jnp.where(hit, 1.0, 0.0), axis=0, keepdims=True)
        hot_at = jnp.sum(
            jnp.where(hit, iota((hot_count, n), 0).astype(F32), 0.0), axis=0, keepdims=True
        )
        owner = lax.shift_right_logical(ids, shift)
        row = ids & ((1 << shift) - 1)
        of_cold = jnp.where(is_hot > 0.5, -1, owner)
        member = (iota((owners, n), 0) == of_cold).astype(F32)
        member_low = member.astype(BF16)
        earlier = (iota((n, n), 0) < iota((n, n), 1)).astype(F32).astype(BF16)
        before = dot(member_low, earlier)
        rank = jnp.sum(before * member, axis=0, keepdims=True)
        slot = rank + first
        here = iota((LANES, n), 0).astype(F32) == slot
        high = jnp.where(here, lax.shift_right_logical(row, 5).astype(F32), 0.0).astype(BF16)
        low = jnp.where(here, (row & 31).astype(F32), 0.0).astype(BF16)
        total = total + 32.0 * dot_nt(member_low, high) + dot_nt(member_low, low)
        cold_at = owner.astype(F32) * SLOTS + rank
        picks[side : side + 1, :] = jnp.where(is_hot > 0.5, owners * SLOTS + hot_at, cold_at)
    asked[...] = total.astype(I32)


def ask(hist_ids, cand_ids, hot_ids, owners, shift):
    n = hist_ids.shape[1]
    return pl.pallas_call(
        lambda *refs: ask_kernel(*refs, owners=owners, shift=shift),
        out_shape=(
            jax.ShapeDtypeStruct((owners, LANES), I32),
            jax.ShapeDtypeStruct((2, n), F32),
        ),
        compiler_params=pltpu.CompilerParams(vmem_limit_bytes=VMEM_BYTES),
        cost_estimate=pl.CostEstimate(flops=10**9, bytes_accessed=10**5, transcendentals=0),
        name="ask",
    )(hist_ids, cand_ids, hot_ids)


def columns_kernel(picks, columns):
    columns[:, 0:1] = to_column(picks[0:1, :])
    columns[:, 1:2] = to_column(picks[1:2, :])


def columns_of(picks):
    n = picks.shape[1]
    return pl.pallas_call(
        columns_kernel,
        out_shape=jax.ShapeDtypeStruct((n, 2), F32),
        compiler_params=pltpu.CompilerParams(vmem_limit_bytes=VMEM_BYTES),
        cost_estimate=pl.CostEstimate(flops=10**8, bytes_accessed=10**5, transcendentals=0),
        name="columns",
    )(picks)


def fetch_kernel(numbers, table, sent, *, first):
    owners = numbers.shape[0]
    rows, width = table.shape
    count = owners * SLOTS
    n = numbers[...]
    spread = (lax.shift_right_logical(iota((count, owners), 0), 2) == iota((count, owners), 1))
    spread = spread.astype(F32).astype(BF16)
    high = lax.shift_right_logical(n, 5).astype(F32).astype(BF16)
    low = (n & 31).astype(F32).astype(BF16)
    every = 32.0 * dot(spread, high) + dot(spread, low)
    lane = iota((count, LANES), 1) == (iota((count, LANES), 0) & (SLOTS - 1)) + first
    number = jnp.sum(jnp.where(lane, every, 0.0), axis=1, keepdims=True).astype(I32)
    chosen = (iota((count, rows), 1) == number).astype(F32).astype(BF16)
    half = width // 2
    left = dot(chosen, table[:, :half]).reshape(owners // 2, 8, half)
    right = dot(chosen, table[:, half:]).reshape(owners // 2, 8, half)
    upper = iota(left.shape, 1) < 4
    even = jnp.where(upper, left, pltpu.roll(right, 4, 1))
    odd = jnp.where(upper, pltpu.roll(left, 4, 1), right)
    sent[:, 0] = even.astype(BF16)
    sent[:, 1] = odd.astype(BF16)


def fetch(numbers, table, first):
    owners = numbers.shape[0]
    rows, width = table.shape
    sent = pl.pallas_call(
        lambda *refs: fetch_kernel(*refs, first=first),
        out_shape=jax.ShapeDtypeStruct((owners // 2, 2, 8, width // 2), BF16),
        compiler_params=pltpu.CompilerParams(vmem_limit_bytes=VMEM_BYTES),
        cost_estimate=pl.CostEstimate(
            flops=3 * 10**9, bytes_accessed=3 * 10**6, transcendentals=0
        ),
        name="fetch",
    )(numbers, table)
    return sent.reshape(owners, 8, width // 2)


def picked_rows(replies, hot, column):
    pairs, _, _, half = replies.shape
    even = replies[:, 0].astype(F32)
    odd = replies[:, 1].astype(F32)
    upper = iota(even.shape, 1) < 4
    left = jnp.where(upper, even, pltpu.roll(odd, 4, 1)).reshape(pairs * 8, half).astype(BF16)
    right = jnp.where(upper, pltpu.roll(even, 4, 1), odd).reshape(pairs * 8, half).astype(BF16)
    n = column.shape[0]
    count = pairs * 8
    at = column.astype(I32)
    cold = (iota((n, count), 1) == at).astype(F32).astype(BF16)
    warm = (iota((n, hot.shape[0]), 1) == at - count).astype(F32).astype(BF16)
    found = jnp.concatenate([dot(cold, left), dot(cold, right)], axis=1)
    return found + dot(warm, hot[...])


def encode_kernel(replies, hot, columns, w_in, gain, x_out, u_out, q_out, kv_out):
    width = hot.shape[1]
    x = picked_rows(replies, hot, columns[:, 0:1])
    x_out[...] = x.astype(BF16)
    inner = norm(x, gain[...]).astype(BF16)
    u_out[...] = silu(dot(inner, w_in[:, :width]))
    kv_out[:, width:] = silu(dot(inner, w_in[:, width : 2 * width])).astype(BF16)
    q_out[...] = silu(dot(inner, w_in[:, 2 * width : 3 * width])).astype(BF16)
    kv_out[:, :width] = silu(dot(inner, w_in[:, 3 * width :])).astype(BF16)


def encode(replies, hot, columns, w_in, gain):
    n = columns.shape[0]
    width = hot.shape[1]
    owners = replies.shape[0]
    return pl.pallas_call(
        encode_kernel,
        out_shape=(
            jax.ShapeDtypeStruct((n, width), BF16),
            jax.ShapeDtypeStruct((n, width), F32),
            jax.ShapeDtypeStruct((n, width), BF16),
            jax.ShapeDtypeStruct((n, 2 * width), BF16),
        ),
        compiler_params=pltpu.CompilerParams(vmem_limit_bytes=VMEM_BYTES),
        cost_estimate=pl.CostEstimate(
            flops=3 * 10**9, bytes_accessed=7 * 10**6, transcendentals=10**6
        ),
        name="encode",
    )(replies.reshape(owners // 2, 2, 8, width // 2), hot, columns, w_in, gain)


def weighed(q, k, v, head_dim, keep=None):
    s = dot_nt(q, k) * (0.5 / head_dim**0.5)
    w = s + s * jnp.tanh(s)
    if keep is not None:
        w = jnp.where(keep, w, 0.0)
    return dot(w.astype(BF16), v)


def finish(mix, gain, u, w_out, x):
    gated = (norm(mix, gain) * u).astype(BF16)
    return (x + dot(gated, w_out)).astype(BF16)


def history_kernel(user, x, u, q, own, other, gain, w_out, out, mix):
    n, width = x.shape
    head_dim = width // HEADS
    causal = iota((n, n), 1) <= iota((n, n), 0)
    for h in range(HEADS):
        at = slice(h * head_dim, (h + 1) * head_dim)
        past = slice(width + h * head_dim, width + (h + 1) * head_dim)
        mix[:, at] = weighed(q[:, at], own[:, at], own[:, past], head_dim, causal)

    @pl.when(user[0] == 1)
    def _():
        for h in range(HEADS):
            at = slice(h * head_dim, (h + 1) * head_dim)
            past = slice(width + h * head_dim, width + (h + 1) * head_dim)
            mix[:, at] += weighed(q[:, at], other[:, at], other[:, past], head_dim)

    out[...] = finish(mix[...], gain[...], u[...], w_out[...], x[...].astype(F32))


def history(user, x, u, q, own, other, gain, w_out):
    vmem = pl.BlockSpec(memory_space=pltpu.VMEM)
    return pl.pallas_call(
        history_kernel,
        out_shape=jax.ShapeDtypeStruct(x.shape, BF16),
        in_specs=[pl.BlockSpec(memory_space=pltpu.SMEM)] + [vmem] * 7,
        out_specs=vmem,
        scratch_shapes=[pltpu.VMEM(x.shape, F32)],
        compiler_params=pltpu.CompilerParams(vmem_limit_bytes=VMEM_BYTES),
        cost_estimate=pl.CostEstimate(
            flops=2 * 10**9, bytes_accessed=5 * 10**6, transcendentals=2 * 10**6
        ),
        name="history",
    )(user, x, u, q, own, other, gain, w_out)


def candidates_kernel(
    replies, hot, columns, w_in, in_gain, own, other, gain, w_out, _, out, mix
):
    width = hot.shape[1]
    head_dim = width // HEADS
    x = picked_rows(replies, hot, columns[:, 1:2])
    inner = norm(x, in_gain[...]).astype(BF16)
    u = silu(dot(inner, w_in[:, :width]))
    q = silu(dot(inner, w_in[:, 2 * width : 3 * width])).astype(BF16)
    for h in range(HEADS):
        at = slice(h * head_dim, (h + 1) * head_dim)
        past = slice(width + h * head_dim, width + (h + 1) * head_dim)
        mix[:, at] = weighed(q[:, at], own[:, at], own[:, past], head_dim) + weighed(
            q[:, at], other[:, at], other[:, past], head_dim
        )
    out[...] = finish(mix[...], gain[...], u, w_out[...], x)


def candidates(replies, hot, columns, w_in, in_gain, own, other, gain, w_out, after):
    n = columns.shape[0]
    width = hot.shape[1]
    owners = replies.shape[0]
    return pl.pallas_call(
        candidates_kernel,
        out_shape=jax.ShapeDtypeStruct((n, width), BF16),
        in_specs=[pl.BlockSpec(memory_space=pltpu.VMEM)] * 9
        + [pl.BlockSpec(memory_space=pl.ANY)],
        out_specs=pl.BlockSpec(memory_space=pltpu.VMEM),
        scratch_shapes=[pltpu.VMEM((n, width), F32)],
        compiler_params=pltpu.CompilerParams(vmem_limit_bytes=VMEM_BYTES),
        cost_estimate=pl.CostEstimate(
            flops=4 * 10**9, bytes_accessed=7 * 10**6, transcendentals=3 * 10**6
        ),
        name="candidates",
    )(
        replies.reshape(owners // 2, 2, 8, width // 2),
        hot,
        columns,
        w_in,
        in_gain,
        own,
        other,
        gain,
        w_out,
        after,
    )


def exchange(array):
    return lax.all_to_all(array, ("req", "cand"), 0, 0, tiled=True)


def per_device(table, hot_table, hot_ids, hist_ids, cand_ids, w_in, w_out, in_gain, attn_gain):
    owners = lax.axis_size("req") * lax.axis_size("cand")
    shift = (table.shape[0] - 1).bit_length()
    asked, picks = ask(hist_ids, cand_ids, hot_ids[None], owners, shift)
    numbers = exchange(asked[:, None, :])[:, 0, :]
    hist_replies = exchange(fetch(numbers, table, 0))
    cand_replies = exchange(fetch(numbers, table, SLOTS))
    columns = columns_of(picks)
    x, u, q, own = encode(hist_replies, hot_table, columns, w_in[0], in_gain)
    other = lax.ppermute(own, "user", [(0, 1), (1, 0)])
    user = lax.axis_index("user")[None].astype(I32)
    hist_out = history(user, x, u, q, own, other, attn_gain, w_out[0])
    cand_out = candidates(
        cand_replies,
        hot_table,
        columns,
        w_in[0],
        in_gain,
        own,
        other,
        attn_gain,
        w_out[0],
        hist_out,
    )
    return hist_out[None], cand_out[None]


def solution(mesh):
    rows = P(("req", "cand"), None)
    split = P(("req", "cand"), "user")
    in_specs = (rows, P(), P(), split, split, P(), P(), P(), P())
    out_specs = (P(("req", "cand"), "user", None), P(("req", "cand"), "user", None))
    return jax.shard_map(
        per_device, mesh=mesh, in_specs=in_specs, out_specs=out_specs, check_vma=False
    )
```

```python
import jax
import jax.numpy as jnp
from jax import lax
from jax.experimental import pallas as pl
from jax.experimental.pallas import tpu as pltpu
from jax.sharding import PartitionSpec as P

HEADS = 4
SLOTS = 4
LANES = 8
F32 = jnp.float32
BF16 = jnp.bfloat16
I32 = jnp.int32
VMEM_BYTES = 20 * 1024 * 1024


def iota(shape, dim):
    return lax.broadcasted_iota(I32, shape, dim)


def dot(a, b):
    return jnp.dot(a, b, preferred_element_type=F32)


def dot_nt(a, b):
    return lax.dot_general(a, b, (((1,), (1,)), ((), ())), preferred_element_type=F32)


def to_column(row):
    n = row.shape[1]
    diag = iota((n, n), 0) == iota((n, n), 1)
    return jnp.sum(jnp.where(diag, row, 0.0), axis=1, keepdims=True)


def silu(v):
    half = 0.5 * v
    return half + half * jnp.tanh(half)


def norm(z, gain):
    centred = z - jnp.mean(z, axis=1, keepdims=True)
    variance = jnp.mean(centred * centred, axis=1, keepdims=True)
    return centred * lax.rsqrt(variance + 1e-05) * gain


def ask_kernel(hist_ids, cand_ids, hot_ids, asked, picks, *, owners, shift):
    hot_count = hot_ids.shape[1]
    hot_column = to_column(hot_ids[...].astype(F32))
    total = jnp.zeros((owners, LANES), F32)
    for side, (ids_ref, first) in enumerate(((hist_ids, 0), (cand_ids, SLOTS))):
        ids = ids_ref[...]
        n = ids.shape[1]
        hit = hot_column == ids.astype(F32)
        is_hot = jnp.max(jnp.where(hit, 1.0, 0.0), axis=0, keepdims=True)
        hot_at = jnp.sum(
            jnp.where(hit, iota((hot_count, n), 0).astype(F32), 0.0), axis=0, keepdims=True
        )
        owner = lax.shift_right_logical(ids, shift)
        row = ids & ((1 << shift) - 1)
        of_cold = jnp.where(is_hot > 0.5, -1, owner)
        member = (iota((owners, n), 0) == of_cold).astype(F32)
        member_low = member.astype(BF16)
        earlier = (iota((n, n), 0) < iota((n, n), 1)).astype(F32).astype(BF16)
        before = dot(member_low, earlier)
        rank = jnp.sum(before * member, axis=0, keepdims=True)
        slot = rank + first
        here = iota((LANES, n), 0).astype(F32) == slot
        high = jnp.where(here, lax.shift_right_logical(row, 5).astype(F32), 0.0).astype(BF16)
        low = jnp.where(here, (row & 31).astype(F32), 0.0).astype(BF16)
        total = total + 32.0 * dot_nt(member_low, high) + dot_nt(member_low, low)
        cold_at = owner.astype(F32) * SLOTS + rank
        picks[side : side + 1, :] = jnp.where(is_hot > 0.5, owners * SLOTS + hot_at, cold_at)
    asked[...] = total.astype(I32)


def ask(hist_ids, cand_ids, hot_ids, owners, shift):
    n = hist_ids.shape[1]
    return pl.pallas_call(
        lambda *refs: ask_kernel(*refs, owners=owners, shift=shift),
        out_shape=(
            jax.ShapeDtypeStruct((owners, LANES), I32),
            jax.ShapeDtypeStruct((2, n), F32),
        ),
        compiler_params=pltpu.CompilerParams(vmem_limit_bytes=VMEM_BYTES),
        cost_estimate=pl.CostEstimate(flops=10**9, bytes_accessed=10**5, transcendentals=0),
        name="ask",
    )(hist_ids, cand_ids, hot_ids)


def columns_kernel(picks, columns):
    columns[:, 0:1] = to_column(picks[0:1, :])
    columns[:, 1:2] = to_column(picks[1:2, :])


def columns_of(picks):
    n = picks.shape[1]
    return pl.pallas_call(
        columns_kernel,
        out_shape=jax.ShapeDtypeStruct((n, 2), F32),
        compiler_params=pltpu.CompilerParams(vmem_limit_bytes=VMEM_BYTES),
        cost_estimate=pl.CostEstimate(flops=10**8, bytes_accessed=10**5, transcendentals=0),
        name="columns",
    )(picks)


def number_column(numbers, first):
    owners = numbers.shape[0]
    count = owners * SLOTS
    spread = lax.shift_right_logical(iota((count, owners), 0), 2) == iota((count, owners), 1)
    spread = spread.astype(F32).astype(BF16)
    high = lax.shift_right_logical(numbers, 5).astype(F32).astype(BF16)
    low = (numbers & 31).astype(F32).astype(BF16)
    every = 32.0 * dot(spread, high) + dot(spread, low)
    place = iota((count, LANES), 0) & (SLOTS - 1)
    columns = []
    for start in first:
        lane = iota((count, LANES), 1) == place + start
        columns.append(jnp.sum(jnp.where(lane, every, 0.0), axis=1, keepdims=True).astype(I32))
    return columns


def one_hot(column, width):
    hit = iota((column.shape[0], width), 1) == column
    return hit.astype(F32).astype(BF16)


def fetch_kernel(numbers, table, sent):
    owners = numbers.shape[0]
    rows, width = table.shape
    count = owners * SLOTS
    cut = width - width // 4
    n = numbers[...]
    hist, cand = number_column(n, (0, SLOTS))
    last = (iota((count, 1), 0) & (SLOTS - 1)) == SLOTS - 1
    cand = jnp.where(last, -1, cand)
    ends = [
        dot(one_hot(n[:, SLOTS + s : SLOTS + s + 1], rows), table[:, cut:])
        for s in range(SLOTS - 1)
    ]
    ends = jnp.concatenate(ends, axis=1).astype(BF16)
    rank = iota((count, owners), 0) - (SLOTS - 1)
    place = (rank == SLOTS * iota((count, owners), 1)).astype(F32).astype(BF16)
    both = dot(one_hot(cand, rows), table[:, :cut]) + dot(place, ends)
    sent[:, :, width:] = both.reshape(owners, SLOTS, cut).astype(BF16)
    whole = dot(one_hot(hist, rows), table[...])
    sent[:, :, :width] = whole.reshape(owners, SLOTS, width).astype(BF16)


def fetch(numbers, table):
    owners = numbers.shape[0]
    rows, width = table.shape
    return pl.pallas_call(
        fetch_kernel,
        out_shape=jax.ShapeDtypeStruct((owners, SLOTS, 2 * width - width // 4), BF16),
        compiler_params=pltpu.CompilerParams(vmem_limit_bytes=VMEM_BYTES),
        cost_estimate=pl.CostEstimate(
            flops=3 * 10**9, bytes_accessed=3 * 10**6, transcendentals=0
        ),
        name="fetch",
    )(numbers, table)


def picked_hist(replies, hot, column):
    owners, _, _ = replies.shape
    width = hot.shape[1]
    count = owners * SLOTS
    dense = replies[:, :, :width].astype(F32).reshape(count, width).astype(BF16)
    at = column.astype(I32)
    return dot(one_hot(at, count), dense) + dot(one_hot(at - count, hot.shape[0]), hot[...])


def picked_cand(replies, hot, column):
    owners, _, _ = replies.shape
    width = hot.shape[1]
    count = owners * SLOTS
    part = width // 4
    cut = width - part
    dense = replies[:, :, width:].astype(F32).reshape(count, cut).astype(BF16)
    at = column.astype(I32)
    slot = at & (SLOTS - 1)
    warm = dot(one_hot(at - count, hot.shape[0]), hot[...])
    begin = dot(one_hot(at, count), dense) + warm[:, :cut]
    ends = dot(one_hot(at | (SLOTS - 1), count), dense)
    end = jnp.where(slot == 0, ends[:, :part], ends[:, 2 * part :])
    end = jnp.where(slot == 1, ends[:, part : 2 * part], end)
    end = jnp.where(at < count, end, warm[:, cut:])
    return jnp.concatenate([begin, end], axis=1)


def keys_kernel(replies, hot, columns, w_in, gain, x_out, in_out, kv_out):
    width = hot.shape[1]
    x = picked_hist(replies, hot, columns[:, 0:1])
    x_out[...] = x.astype(BF16)
    inner = norm(x, gain[...]).astype(BF16)
    in_out[...] = inner
    kv_out[:, width:] = silu(dot(inner, w_in[:, width : 2 * width])).astype(BF16)
    kv_out[:, :width] = silu(dot(inner, w_in[:, 3 * width :])).astype(BF16)


def keys(replies, hot, columns, w_in, gain):
    n = columns.shape[0]
    width = hot.shape[1]
    return pl.pallas_call(
        keys_kernel,
        out_shape=(
            jax.ShapeDtypeStruct((n, width), BF16),
            jax.ShapeDtypeStruct((n, width), BF16),
            jax.ShapeDtypeStruct((n, 2 * width), BF16),
        ),
        compiler_params=pltpu.CompilerParams(vmem_limit_bytes=VMEM_BYTES),
        cost_estimate=pl.CostEstimate(
            flops=2 * 10**9, bytes_accessed=5 * 10**6, transcendentals=10**6
        ),
        name="keys",
    )(replies, hot, columns, w_in, gain)


def queries_kernel(
    replies, hot, columns, inner, w_in, gain, y_out, hist_u, hist_q, cand_u, cand_q
):
    width = hot.shape[1]
    y = picked_cand(replies, hot, columns[:, 1:2])
    y_out[...] = y.astype(BF16)
    cand_in = norm(y, gain[...]).astype(BF16)
    w_u = w_in[:, :width]
    w_q = w_in[:, 2 * width : 3 * width]
    cand_u[...] = silu(dot(cand_in, w_u))
    cand_q[...] = silu(dot(cand_in, w_q)).astype(BF16)
    hist_u[...] = silu(dot(inner[...], w_u))
    hist_q[...] = silu(dot(inner[...], w_q)).astype(BF16)


def queries(replies, hot, columns, inner, w_in, gain):
    n = columns.shape[0]
    width = hot.shape[1]
    return pl.pallas_call(
        queries_kernel,
        out_shape=(
            jax.ShapeDtypeStruct((n, width), BF16),
            jax.ShapeDtypeStruct((n, width), F32),
            jax.ShapeDtypeStruct((n, width), BF16),
            jax.ShapeDtypeStruct((n, width), F32),
            jax.ShapeDtypeStruct((n, width), BF16),
        ),
        compiler_params=pltpu.CompilerParams(vmem_limit_bytes=VMEM_BYTES),
        cost_estimate=pl.CostEstimate(
            flops=3 * 10**9, bytes_accessed=7 * 10**6, transcendentals=10**6
        ),
        name="queries",
    )(replies, hot, columns, inner, w_in, gain)


def weighed(q, k, v, head_dim, keep=None):
    s = dot_nt(q, k) * (0.5 / head_dim**0.5)
    w = s + s * jnp.tanh(s)
    if keep is not None:
        w = jnp.where(keep, w, 0.0)
    return dot(w.astype(BF16), v)


def finish(mix, gain, u, w_out, x):
    gated = (norm(mix, gain) * u).astype(BF16)
    return (x + dot(gated, w_out)).astype(BF16)


def mix_kernel(
    user, x, y, hist_u, hist_q, cand_u, cand_q, own, other, gain, w_out, hist_out, cand_out, mix, cand_mix
):
    n, width = x.shape
    head_dim = width // HEADS
    causal = iota((n, n), 1) <= iota((n, n), 0)
    for h in range(HEADS):
        at = slice(h * head_dim, (h + 1) * head_dim)
        past = slice(width + h * head_dim, width + (h + 1) * head_dim)
        mix[:, at] = weighed(hist_q[:, at], own[:, at], own[:, past], head_dim, causal)
        cand_mix[:, at] = weighed(
            cand_q[:, at], own[:, at], own[:, past], head_dim
        ) + weighed(cand_q[:, at], other[:, at], other[:, past], head_dim)

    @pl.when(user[0] == 1)
    def _():
        for h in range(HEADS):
            at = slice(h * head_dim, (h + 1) * head_dim)
            past = slice(width + h * head_dim, width + (h + 1) * head_dim)
            mix[:, at] += weighed(hist_q[:, at], other[:, at], other[:, past], head_dim)

    hist_out[...] = finish(mix[...], gain[...], hist_u[...], w_out[...], x[...].astype(F32))
    cand_out[...] = finish(
        cand_mix[...], gain[...], cand_u[...], w_out[...], y[...].astype(F32)
    )


def mixed(user, x, y, hist_u, hist_q, cand_u, cand_q, own, other, gain, w_out):
    vmem = pl.BlockSpec(memory_space=pltpu.VMEM)
    return pl.pallas_call(
        mix_kernel,
        out_shape=(jax.ShapeDtypeStruct(x.shape, BF16), jax.ShapeDtypeStruct(y.shape, BF16)),
        in_specs=[pl.BlockSpec(memory_space=pltpu.SMEM)] + [vmem] * 10,
        out_specs=(vmem, vmem),
        scratch_shapes=[pltpu.VMEM(x.shape, F32), pltpu.VMEM(y.shape, F32)],
        compiler_params=pltpu.CompilerParams(vmem_limit_bytes=VMEM_BYTES),
        cost_estimate=pl.CostEstimate(
            flops=4 * 10**9, bytes_accessed=7 * 10**6, transcendentals=4 * 10**6
        ),
        name="mix",
    )(user, x, y, hist_u, hist_q, cand_u, cand_q, own, other, gain, w_out)


def exchange(array):
    return lax.all_to_all(array, ("req", "cand"), 0, 0, tiled=True)


def per_device(table, hot_table, hot_ids, hist_ids, cand_ids, w_in, w_out, in_gain, attn_gain):
    owners = lax.axis_size("req") * lax.axis_size("cand")
    shift = (table.shape[0] - 1).bit_length()
    asked, picks = ask(hist_ids, cand_ids, hot_ids[None], owners, shift)
    numbers = exchange(asked[:, None, :])[:, 0, :]
    replies = exchange(fetch(numbers, table))
    columns = columns_of(picks)
    x, inner, own = keys(replies, hot_table, columns, w_in[0], in_gain)
    other = lax.ppermute(own, "user", [(0, 1), (1, 0)])
    y, hist_u, hist_q, cand_u, cand_q = queries(
        replies, hot_table, columns, inner, w_in[0], in_gain
    )
    user = lax.axis_index("user")[None].astype(I32)
    hist_out, cand_out = mixed(
        user, x, y, hist_u, hist_q, cand_u, cand_q, own, other, attn_gain, w_out[0]
    )
    return hist_out[None], cand_out[None]


def solution(mesh):
    rows = P(("req", "cand"), None)
    split = P(("req", "cand"), "user")
    in_specs = (rows, P(), P(), split, split, P(), P(), P(), P())
    out_specs = (P(("req", "cand"), "user", None), P(("req", "cand"), "user", None))
    return jax.shard_map(
        per_device, mesh=mesh, in_specs=in_specs, out_specs=out_specs, check_vma=False
    )
```

```python
import jax
import jax.numpy as jnp
from jax import lax
from jax.experimental import pallas as pl
from jax.experimental.pallas import tpu as pltpu
from jax.sharding import PartitionSpec as P

HEADS = 4
SLOTS = 4
LANES = 8
FETCH_PARTS = 2
F32 = jnp.float32
BF16 = jnp.bfloat16
I32 = jnp.int32
ASK_BYTES = 63 * 1024 * 1024
VMEM_BYTES = 62 * 1024 * 1024
COLUMN_BYTES = 60 * 1024 * 1024
HBM = pl.BlockSpec(memory_space=pltpu.HBM)
VMEM = pl.BlockSpec(memory_space=pltpu.VMEM)
SMEM = pl.BlockSpec(memory_space=pltpu.SMEM)
KEYS_BYTES = 63 * 1024 * 1024
LAYER_BYTES = 62 * 1024 * 1024 + 512 * 1024
DMA = pltpu.SemaphoreType.DMA


def iota(shape, dim):
    return lax.broadcasted_iota(I32, shape, dim)


def dot(a, b):
    return jnp.dot(a, b, preferred_element_type=F32)


def dot_nt(a, b):
    return lax.dot_general(a, b, (((1,), (1,)), ((), ())), preferred_element_type=F32)


def to_column(row):
    n = row.shape[1]
    diag = iota((n, n), 0) == iota((n, n), 1)
    return jnp.sum(jnp.where(diag, row, 0.0), axis=1, keepdims=True)


def silu(v):
    half = 0.5 * v
    return half + half * jnp.tanh(half)


def norm(z, gain):
    centred = z - jnp.mean(z, axis=1, keepdims=True)
    variance = jnp.mean(centred * centred, axis=1, keepdims=True)
    return centred * lax.rsqrt(variance + 1e-05) * gain


def started(pairs, sems):
    copies = [pltpu.make_async_copy(a, b, sems.at[i]) for i, (a, b) in enumerate(pairs)]
    for copy in copies:
        copy.start()
    return copies


def ask_kernel(hist_in, cand_in, hot_in, asked, picks, hist_ids, cand_ids, hot_ids, sems, *, owners, shift):
    pairs = ((hot_in, hot_ids), (hist_in, hist_ids), (cand_in, cand_ids))
    for copy in started(pairs, sems):
        copy.wait()
    hot_count = hot_ids.shape[1]
    hot_column = to_column(hot_ids[...].astype(F32))
    total = jnp.zeros((owners, LANES), F32)
    for side, (ids_ref, first) in enumerate(((hist_ids, 0), (cand_ids, SLOTS))):
        ids = ids_ref[...]
        n = ids.shape[1]
        hit = hot_column == ids.astype(F32)
        is_hot = jnp.max(jnp.where(hit, 1.0, 0.0), axis=0, keepdims=True)
        hot_at = jnp.sum(
            jnp.where(hit, iota((hot_count, n), 0).astype(F32), 0.0), axis=0, keepdims=True
        )
        owner = lax.shift_right_logical(ids, shift)
        row = ids & ((1 << shift) - 1)
        of_cold = jnp.where(is_hot > 0.5, -1, owner)
        member = (iota((owners, n), 0) == of_cold).astype(F32)
        member_low = member.astype(BF16)
        earlier = (iota((n, n), 0) < iota((n, n), 1)).astype(F32).astype(BF16)
        before = dot(member_low, earlier)
        rank = jnp.sum(before * member, axis=0, keepdims=True)
        slot = rank + first
        here = iota((LANES, n), 0).astype(F32) == slot
        high = jnp.where(here, lax.shift_right_logical(row, 5).astype(F32), 0.0).astype(BF16)
        low = jnp.where(here, (row & 31).astype(F32), 0.0).astype(BF16)
        total = total + 32.0 * dot_nt(member_low, high) + dot_nt(member_low, low)
        cold_at = owner.astype(F32) * SLOTS + rank
        picks[side : side + 1, :] = jnp.where(is_hot > 0.5, owners * SLOTS + hot_at, cold_at)
    asked[...] = total.astype(I32)


def ask(hist_ids, cand_ids, hot_ids, owners, shift):
    n = hist_ids.shape[1]
    return pl.pallas_call(
        lambda *refs: ask_kernel(*refs, owners=owners, shift=shift),
        out_shape=(
            jax.ShapeDtypeStruct((owners, LANES), I32),
            jax.ShapeDtypeStruct((2, n), F32),
        ),
        in_specs=[HBM] * 3,
        out_specs=(VMEM, VMEM),
        scratch_shapes=[
            pltpu.VMEM((1, n), I32),
            pltpu.VMEM((1, n), I32),
            pltpu.VMEM(hot_ids.shape, I32),
            DMA((3,)),
        ],
        compiler_params=pltpu.CompilerParams(vmem_limit_bytes=ASK_BYTES),
        cost_estimate=pl.CostEstimate(flops=10**9, bytes_accessed=10**5, transcendentals=0),
        name="ask",
    )(hist_ids, cand_ids, hot_ids)


def columns_kernel(picks, columns):
    columns[:, 0:1] = to_column(picks[0:1, :])
    columns[:, 1:2] = to_column(picks[1:2, :])


def columns_of(picks):
    n = picks.shape[1]
    return pl.pallas_call(
        columns_kernel,
        out_shape=jax.ShapeDtypeStruct((n, 2), F32),
        compiler_params=pltpu.CompilerParams(vmem_limit_bytes=COLUMN_BYTES),
        cost_estimate=pl.CostEstimate(flops=10**8, bytes_accessed=10**5, transcendentals=0),
        name="columns",
    )(picks)


def number_column(numbers, first):
    owners = numbers.shape[0]
    count = owners * SLOTS
    spread = lax.shift_right_logical(iota((count, owners), 0), 2) == iota((count, owners), 1)
    spread = spread.astype(F32).astype(BF16)
    high = lax.shift_right_logical(numbers, 5).astype(F32).astype(BF16)
    low = (numbers & 31).astype(F32).astype(BF16)
    every = 32.0 * dot(spread, high) + dot(spread, low)
    place = iota((count, LANES), 0) & (SLOTS - 1)
    columns = []
    for start in first:
        lane = iota((count, LANES), 1) == place + start
        columns.append(jnp.sum(jnp.where(lane, every, 0.0), axis=1, keepdims=True).astype(I32))
    return columns


def one_hot(column, width):
    hit = iota((column.shape[0], width), 1) == column
    return hit.astype(F32).astype(BF16)


def fetch_kernel(numbers, table_in, out, table, sent, sems):
    owners = numbers.shape[0]
    rows, width = table.shape
    (arrival,) = started(((table_in, table),), sems.at[pl.ds(FETCH_PARTS, 1)])
    cut = width - width // 4
    n = numbers[...]
    hist, cand = number_column(n, (0, SLOTS))
    arrival.wait()
    copies = []
    for part in range(FETCH_PARTS):
        step = owners // FETCH_PARTS
        count = step * SLOTS
        mine = slice(part * step, (part + 1) * step)
        wide = slice(part * count, (part + 1) * count)
        last = (iota((count, 1), 0) & (SLOTS - 1)) == SLOTS - 1
        ends = [
            dot(one_hot(n[mine, SLOTS + s : SLOTS + s + 1], rows), table[:, cut:])
            for s in range(SLOTS - 1)
        ]
        ends = jnp.concatenate(ends, axis=1).astype(BF16)
        rank = iota((count, step), 0) - (SLOTS - 1)
        place = (rank == SLOTS * iota((count, step), 1)).astype(F32).astype(BF16)
        begin = dot(one_hot(jnp.where(last, -1, cand[wide]), rows), table[:, :cut])
        both = begin + dot(place, ends)
        sent[mine, :, width:] = both.reshape(step, SLOTS, cut).astype(BF16)
        whole = dot(one_hot(hist[wide], rows), table[...])
        sent[mine, :, :width] = whole.reshape(step, SLOTS, width).astype(BF16)
        copies.append(pltpu.make_async_copy(sent.at[mine], out.at[mine], sems.at[part]))
        copies[-1].start()
    for copy in copies:
        copy.wait()


def fetch(numbers, table):
    owners = numbers.shape[0]
    rows, width = table.shape
    shape = (owners, SLOTS, 2 * width - width // 4)
    return pl.pallas_call(
        fetch_kernel,
        out_shape=jax.ShapeDtypeStruct(shape, BF16),
        in_specs=[VMEM, HBM],
        out_specs=HBM,
        scratch_shapes=[
            pltpu.VMEM(table.shape, BF16),
            pltpu.VMEM(shape, BF16),
            DMA((FETCH_PARTS + 1,)),
        ],
        compiler_params=pltpu.CompilerParams(vmem_limit_bytes=VMEM_BYTES),
        cost_estimate=pl.CostEstimate(
            flops=3 * 10**9, bytes_accessed=3 * 10**6, transcendentals=0
        ),
        name="fetch",
    )(numbers, table)


def picked_hist(replies, hot, column, arrival):
    owners, _, width = replies.shape
    count = owners * SLOTS
    at = column.astype(I32)
    warm = dot(one_hot(at - count, hot.shape[0]), hot[...])
    cold = one_hot(at, count)
    arrival.wait()
    dense = replies[...].astype(F32).reshape(count, width).astype(BF16)
    return dot(cold, dense) + warm


def picked_cand(replies, hot, column, arrival):
    owners, _, cut = replies.shape
    count = owners * SLOTS
    part = hot.shape[1] - cut
    at = column.astype(I32)
    slot = at & (SLOTS - 1)
    warm = dot(one_hot(at - count, hot.shape[0]), hot[...])
    arrival.wait()
    dense = replies[...].astype(F32).reshape(count, cut).astype(BF16)
    begin = dot(one_hot(at, count), dense) + warm[:, :cut]
    ends = dot(one_hot(at | (SLOTS - 1), count), dense)
    end = jnp.where(slot == 0, ends[:, :part], ends[:, 2 * part :])
    end = jnp.where(slot == 1, ends[:, part : 2 * part], end)
    end = jnp.where(at < count, end, warm[:, cut:])
    return jnp.concatenate([begin, end], axis=1)


def keys_kernel(
    hot, columns, gain, replies_in, w_in, x_out, in_out, kv_out,
    replies, x_own, in_own, kv_own, w_v, w_k, sems,
):
    width = hot.shape[1]
    side = pl.ds(0, width)
    (arrival,) = started(((replies_in.at[:, :, side], replies),), sems.at[pl.ds(6, 1)])
    at_v = pl.ds(width, width)
    at_k = pl.ds(3 * width, width)
    v_in, k_in = started(((w_in.at[:, at_v], w_v), (w_in.at[:, at_k], w_k)), sems)
    x = picked_hist(replies, hot, columns[:, 0:1], arrival)
    x_own[...] = x.astype(BF16)
    inner = norm(x, gain[...]).astype(BF16)
    in_own[...] = inner
    done = started(((x_own, x_out), (in_own, in_out)), sems.at[pl.ds(2, 2)])
    v_in.wait()
    kv_own[:, width:] = silu(dot(inner, w_v[...])).astype(BF16)
    lower = pl.ds(0, width)
    done += started(
        ((kv_own.at[:, at_v], kv_out.at[:, at_v]),), sems.at[pl.ds(4, 1)]
    )
    k_in.wait()
    kv_own[:, :width] = silu(dot(inner, w_k[...])).astype(BF16)
    done += started(
        ((kv_own.at[:, lower], kv_out.at[:, lower]),), sems.at[pl.ds(5, 1)]
    )
    for copy in done:
        copy.wait()


def keys(replies, hot, columns, w_in, gain):
    n = columns.shape[0]
    width = hot.shape[1]
    return pl.pallas_call(
        keys_kernel,
        out_shape=(
            jax.ShapeDtypeStruct((n, width), BF16),
            jax.ShapeDtypeStruct((n, width), BF16),
            jax.ShapeDtypeStruct((n, 2 * width), BF16),
        ),
        in_specs=[VMEM] * 3 + [HBM] * 2,
        out_specs=(HBM, HBM, HBM),
        scratch_shapes=[
            pltpu.VMEM((replies.shape[0], SLOTS, width), BF16),
            pltpu.VMEM((n, width), BF16),
            pltpu.VMEM((n, width), BF16),
            pltpu.VMEM((n, 2 * width), BF16),
            pltpu.VMEM((width, width), BF16),
            pltpu.VMEM((width, width), BF16),
            DMA((7,)),
        ],
        compiler_params=pltpu.CompilerParams(vmem_limit_bytes=KEYS_BYTES),
        cost_estimate=pl.CostEstimate(
            flops=2 * 10**9, bytes_accessed=5 * 10**6, transcendentals=10**6
        ),
        name="keys",
    )(hot, columns, gain, replies, w_in)


def weights(q, k, head_dim):
    half = dot_nt(q, k) * (0.5 / head_dim**0.5)
    return half + half * jnp.tanh(half)


def layer_kernel(
    user, hot, columns, in_gain, gain, replies_in, x_in, hist_in, own_in, other_in, w_in, w_last,
    hist_out, cand_out,
    replies, xs, ins, own, other, w_q, w_u, w_out, qs, us, mix, outs, sems,
):
    n, width = x_in.shape
    head_dim = width // HEADS
    hist, cand = pl.ds(0, n), pl.ds(n, n)
    arrival, in_q, in_in, in_u, in_own, in_other, in_out, in_x = started(
        (
            (replies_in.at[:, :, pl.ds(width, replies.shape[2])], replies),
            (w_in.at[:, pl.ds(2 * width, width)], w_q),
            (hist_in, ins.at[hist]),
            (w_in.at[:, pl.ds(0, width)], w_u),
            (own_in, own),
            (other_in, other),
            (w_last, w_out),
            (x_in, xs.at[hist]),
        ),
        sems,
    )
    y = picked_cand(replies, hot, columns[:, 1:2], arrival)
    xs[cand, :] = y.astype(BF16)
    ins[cand, :] = norm(y, in_gain[...]).astype(BF16)
    in_q.wait()
    in_in.wait()
    qs[...] = silu(dot(ins[...], w_q[...])).astype(BF16)
    in_u.wait()
    us[...] = silu(dot(ins[...], w_u[...]))
    in_own.wait()
    in_other.wait()
    causal = iota((n, n), 1) <= iota((n, n), 0)

    def heads(everyone):
        for h in range(HEADS):
            at = slice(h * head_dim, (h + 1) * head_dim)
            past = slice(width + h * head_dim, width + (h + 1) * head_dim)
            near = weights(qs[:, at], own[:, at], head_dim)
            near = jnp.concatenate([jnp.where(causal, near[:n], 0.0), near[n:]], axis=0)
            total = dot(near.astype(BF16), own[:, past])
            if everyone:
                far = weights(qs[:, at], other[:, at], head_dim)
                mix[:, at] = total + dot(far.astype(BF16), other[:, past])
            else:
                far = weights(qs[n:, at], other[:, at], head_dim)
                mix[:n, at] = total[:n]
                mix[n:, at] = total[n:] + dot(far.astype(BF16), other[:, past])

    @pl.when(user[0] == 1)
    def _():
        heads(True)

    @pl.when(user[0] == 0)
    def _():
        heads(False)

    in_out.wait()
    in_x.wait()
    done = []
    for i, (rows, out) in enumerate(((hist, hist_out), (cand, cand_out))):
        gated = (norm(mix[rows, :], gain[...]) * us[rows, :]).astype(BF16)
        outs[rows, :] = (xs[rows, :].astype(F32) + dot(gated, w_out[...])).astype(BF16)
        done += started(((outs.at[rows], out),), sems.at[pl.ds(8 + i, 1)])
    for copy in done:
        copy.wait()


def layer(user, replies, hot, columns, in_gain, gain, x, hist_in, own, other, w_in, w_out):
    n, width = x.shape
    shape = jax.ShapeDtypeStruct(x.shape, BF16)
    return pl.pallas_call(
        layer_kernel,
        out_shape=(shape, shape),
        in_specs=[SMEM] + [VMEM] * 4 + [HBM] * 7,
        out_specs=(HBM, HBM),
        scratch_shapes=[
            pltpu.VMEM((replies.shape[0], SLOTS, replies.shape[2] - width), BF16),
            pltpu.VMEM((2 * n, width), BF16),
            pltpu.VMEM((2 * n, width), BF16),
            pltpu.VMEM((n, 2 * width), BF16),
            pltpu.VMEM((n, 2 * width), BF16),
            pltpu.VMEM((width, width), BF16),
            pltpu.VMEM((width, width), BF16),
            pltpu.VMEM((width, width), BF16),
            pltpu.VMEM((2 * n, width), BF16),
            pltpu.VMEM((2 * n, width), F32),
            pltpu.VMEM((2 * n, width), F32),
            pltpu.VMEM((2 * n, width), BF16),
            DMA((10,)),
        ],
        compiler_params=pltpu.CompilerParams(vmem_limit_bytes=LAYER_BYTES),
        cost_estimate=pl.CostEstimate(
            flops=6 * 10**9, bytes_accessed=9 * 10**6, transcendentals=6 * 10**6
        ),
        name="layer",
    )(user, hot, columns, in_gain, gain, replies, x, hist_in, own, other, w_in, w_out)


def exchange(array):
    return lax.all_to_all(array, ("req", "cand"), 0, 0, tiled=True)


def per_device(table, hot_table, hot_ids, hist_ids, cand_ids, w_in, w_out, in_gain, attn_gain):
    owners = lax.axis_size("req") * lax.axis_size("cand")
    shift = (table.shape[0] - 1).bit_length()
    asked, picks = ask(hist_ids, cand_ids, hot_ids[None], owners, shift)
    numbers = exchange(asked[:, None, :])[:, 0, :]
    replies = exchange(fetch(numbers, table))
    columns = columns_of(picks)
    x, inner, own = keys(replies, hot_table, columns, w_in[0], in_gain)
    other = lax.ppermute(own, "user", [(0, 1), (1, 0)])
    user = lax.axis_index("user")[None].astype(I32)
    hist_out, cand_out = layer(
        user,
        replies,
        hot_table,
        columns,
        in_gain,
        attn_gain,
        x,
        inner,
        own,
        other,
        w_in[0],
        w_out[0],
    )
    return hist_out[None], cand_out[None]


def solution(mesh):
    rows = P(("req", "cand"), None)
    split = P(("req", "cand"), "user")
    in_specs = (rows, P(), P(), split, split, P(), P(), P(), P())
    out_specs = (P(("req", "cand"), "user", None), P(("req", "cand"), "user", None))
    return jax.shard_map(
        per_device, mesh=mesh, in_specs=in_specs, out_specs=out_specs, check_vma=False
    )
```

```python
import jax
import jax.numpy as jnp
from jax import lax
from jax.experimental import pallas as pl
from jax.experimental.pallas import tpu as pltpu
from jax.sharding import PartitionSpec as P

HEADS = 4
SLOTS = 4
LANES = 8
FETCH_PARTS = 2
TABLE_PARTS = 4
SPARE = 16
F32 = jnp.float32
BF16 = jnp.bfloat16
I32 = jnp.int32
ASK_BYTES = 64512 * 1024
VMEM_BYTES = 53248 * 1024
COLUMN_BYTES = 51200 * 1024
HBM = pl.BlockSpec(memory_space=pltpu.HBM)
VMEM = pl.BlockSpec(memory_space=pltpu.VMEM)
SMEM = pl.BlockSpec(memory_space=pltpu.SMEM)
KEYS_BYTES = 50176 * 1024
LAYER_BYTES = 50176 * 1024
DMA = pltpu.SemaphoreType.DMA


def iota(shape, dim):
    return lax.broadcasted_iota(I32, shape, dim)


def dot(a, b):
    return jnp.dot(a, b, preferred_element_type=F32)


def dot_nt(a, b):
    return lax.dot_general(a, b, (((1,), (1,)), ((), ())), preferred_element_type=F32)


def to_column(row):
    n = row.shape[1]
    diag = iota((n, n), 0) == iota((n, n), 1)
    return jnp.sum(jnp.where(diag, row, 0.0), axis=1, keepdims=True)


def silu(v):
    half = 0.5 * v
    return half + half * jnp.tanh(half)


def norm(z, gain):
    centred = z - jnp.mean(z, axis=1, keepdims=True)
    variance = jnp.mean(centred * centred, axis=1, keepdims=True)
    return centred * lax.rsqrt(variance + 1e-05) * gain


def started(pairs, sems):
    copies = [pltpu.make_async_copy(a, b, sems.at[i]) for i, (a, b) in enumerate(pairs)]
    for copy in copies:
        copy.start()
    return copies


def ask_kernel(hist_in, cand_in, hot_in, asked, picks, hist_ids, cand_ids, hot_ids, sems, *, owners, shift):
    pairs = ((hot_in, hot_ids), (hist_in, hist_ids), (cand_in, cand_ids))
    for copy in started(pairs, sems):
        copy.wait()
    hot_count = hot_ids.shape[1]
    hot_column = to_column(hot_ids[...].astype(F32))
    total = jnp.zeros((owners, LANES), F32)
    for side, (ids_ref, first) in enumerate(((hist_ids, 0), (cand_ids, SLOTS))):
        ids = ids_ref[...]
        n = ids.shape[1]
        hit = hot_column == ids.astype(F32)
        is_hot = jnp.max(jnp.where(hit, 1.0, 0.0), axis=0, keepdims=True)
        hot_at = jnp.sum(
            jnp.where(hit, iota((hot_count, n), 0).astype(F32), 0.0), axis=0, keepdims=True
        )
        owner = lax.shift_right_logical(ids, shift)
        row = ids & ((1 << shift) - 1)
        of_cold = jnp.where(is_hot > 0.5, -1, owner)
        member = (iota((owners, n), 0) == of_cold).astype(F32)
        member_low = member.astype(BF16)
        earlier = (iota((n, n), 0) < iota((n, n), 1)).astype(F32).astype(BF16)
        before = dot(member_low, earlier)
        rank = jnp.sum(before * member, axis=0, keepdims=True)
        slot = rank + first
        here = iota((LANES, n), 0).astype(F32) == slot
        high = jnp.where(here, lax.shift_right_logical(row, 5).astype(F32), 0.0).astype(BF16)
        low = jnp.where(here, (row & 31).astype(F32), 0.0).astype(BF16)
        total = total + 32.0 * dot_nt(member_low, high) + dot_nt(member_low, low)
        cold_at = owner.astype(F32) * SLOTS + rank
        picks[side : side + 1, :] = jnp.where(is_hot > 0.5, owners * SLOTS + hot_at, cold_at)
    asked[...] = total.astype(I32)


def ask(hist_ids, cand_ids, hot_ids, owners, shift):
    n = hist_ids.shape[1]
    return pl.pallas_call(
        lambda *refs: ask_kernel(*refs, owners=owners, shift=shift),
        out_shape=(
            jax.ShapeDtypeStruct((owners, LANES), I32),
            jax.ShapeDtypeStruct((2, n), F32),
        ),
        in_specs=[HBM] * 3,
        out_specs=(VMEM, VMEM),
        scratch_shapes=[
            pltpu.VMEM((1, n), I32),
            pltpu.VMEM((1, n), I32),
            pltpu.VMEM(hot_ids.shape, I32),
            DMA((3,)),
        ],
        compiler_params=pltpu.CompilerParams(vmem_limit_bytes=ASK_BYTES),
        cost_estimate=pl.CostEstimate(flops=10**9, bytes_accessed=10**5, transcendentals=0),
        name="ask",
    )(hist_ids, cand_ids, hot_ids)


def number_column(numbers, first):
    owners = numbers.shape[0]
    count = owners * SLOTS
    spread = lax.shift_right_logical(iota((count, owners), 0), 2) == iota((count, owners), 1)
    spread = spread.astype(F32).astype(BF16)
    high = lax.shift_right_logical(numbers, 5).astype(F32).astype(BF16)
    low = (numbers & 31).astype(F32).astype(BF16)
    every = 32.0 * dot(spread, high) + dot(spread, low)
    place = iota((count, LANES), 0) & (SLOTS - 1)
    columns = []
    for start in first:
        lane = iota((count, LANES), 1) == place + start
        columns.append(jnp.sum(jnp.where(lane, every, 0.0), axis=1, keepdims=True).astype(I32))
    return columns


def one_hot(column, width):
    hit = iota((column.shape[0], width), 1) == column
    return hit.astype(F32).astype(BF16)


def fetch_kernel(numbers, table_in, out, table, sent, sems):
    owners = numbers.shape[0]
    rows, width = table.shape
    cut = width - width // 4
    piece = rows // TABLE_PARTS
    pieces = [pl.ds(i * piece, piece) for i in range(TABLE_PARTS)]
    arrivals = started(tuple((table_in.at[p], table.at[p]) for p in pieces), sems)
    hist, cand = number_column(numbers[...], (0, SLOTS))
    step = owners // FETCH_PARTS
    count = step * SLOTS
    place = iota((count, step), 0) - (SLOTS - 1) == SLOTS * iota((count, step), 1)
    place = place.astype(F32).astype(BF16)
    last = (iota((count, 1), 0) & (SLOTS - 1)) == SLOTS - 1
    for arrival in arrivals:
        arrival.wait()
    copies = []
    for part in range(FETCH_PARTS):
        mine = slice(part * step, (part + 1) * step)
        block = pl.ds(part * step, step)
        wide = slice(part * count, (part + 1) * count)
        whole = dot(one_hot(hist[wide], rows), table[...])
        sent[mine, :, :width] = whole.reshape(step, SLOTS, width).astype(BF16)
        first = TABLE_PARTS + 2 * part
        side = pl.ds(0, width)
        copies += started(
            ((sent.at[block, :, side], out.at[block, :, side]),), sems.at[pl.ds(first, 1)]
        )
        ends = [
            dot(one_hot(numbers[mine, SLOTS + s : SLOTS + s + 1], rows), table[:, cut:])
            for s in range(SLOTS - 1)
        ]
        ends = jnp.concatenate(ends, axis=1).astype(BF16)
        begin = dot(one_hot(jnp.where(last, -1, cand[wide]), rows), table[:, :cut])
        both = begin + dot(place, ends)
        sent[mine, :, width:] = both.reshape(step, SLOTS, cut).astype(BF16)
        side = pl.ds(width, cut)
        copies += started(
            ((sent.at[block, :, side], out.at[block, :, side]),), sems.at[pl.ds(first + 1, 1)]
        )
    for copy in copies:
        copy.wait()


def fetch(numbers, table):
    owners = numbers.shape[0]
    rows, width = table.shape
    shape = (owners, SLOTS, 2 * width - width // 4)
    return pl.pallas_call(
        fetch_kernel,
        out_shape=jax.ShapeDtypeStruct(shape, BF16),
        in_specs=[VMEM, HBM],
        out_specs=HBM,
        scratch_shapes=[
            pltpu.VMEM(table.shape, BF16),
            pltpu.VMEM(shape, BF16),
            DMA((TABLE_PARTS + 2 * FETCH_PARTS,)),
        ],
        compiler_params=pltpu.CompilerParams(vmem_limit_bytes=VMEM_BYTES),
        cost_estimate=pl.CostEstimate(
            flops=3 * 10**9, bytes_accessed=3 * 10**6, transcendentals=0
        ),
        name="fetch",
    )(numbers, table)


def picked_hist(replies, hot, column):
    owners = replies.shape[0]
    width = hot.shape[1]
    count = owners * SLOTS
    at = column.astype(I32)
    warm = dot(one_hot(at - count, hot.shape[0]), hot[...])
    cold = one_hot(at, count)
    dense = replies[:, :, :width].astype(F32).reshape(count, width).astype(BF16)
    return dot(cold, dense) + warm


def picked_cand(replies, hot, column):
    owners = replies.shape[0]
    width = hot.shape[1]
    count = owners * SLOTS
    part = width // 4
    cut = width - part
    at = column.astype(I32)
    slot = at & (SLOTS - 1)
    warm = dot(one_hot(at - count, hot.shape[0]), hot[...])
    dense = replies[:, :, width:].astype(F32).reshape(count, cut).astype(BF16)
    begin = dot(one_hot(at, count), dense) + warm[:, :cut]
    ends = dot(one_hot(at | (SLOTS - 1), count), dense)
    end = jnp.where(slot == 0, ends[:, :part], ends[:, 2 * part :])
    end = jnp.where(slot == 1, ends[:, part : 2 * part], end)
    end = jnp.where(at < count, end, warm[:, cut:])
    return jnp.concatenate([begin, end], axis=1)


def keys_kernel(
    hot, picks, gain, replies, w_in, rows_out, kv, x_own, in_own, w_v, w_k, sems
):
    n, width = x_own.shape
    x_out, in_out = rows_out.at[pl.ds(0, n)], rows_out.at[pl.ds(n, n)]
    at_v = pl.ds(width, width)
    at_k = pl.ds(3 * width, width)
    v_in, k_in = started(((w_in.at[:, at_v], w_v), (w_in.at[:, at_k], w_k)), sems)
    x = picked_hist(replies, hot, to_column(picks[0:1, :]))
    x_own[...] = x.astype(BF16)
    inner = norm(x, gain[...]).astype(BF16)
    in_own[...] = inner
    done = started(((x_own, x_out), (in_own, in_out)), sems.at[pl.ds(2, 2)])
    v_in.wait()
    kv[:, width:] = silu(dot(inner, w_v[...])).astype(BF16)
    k_in.wait()
    kv[:, :width] = silu(dot(inner, w_k[...])).astype(BF16)
    for copy in done:
        copy.wait()


def keys(replies, hot, picks, w_in, gain):
    n = picks.shape[1]
    width = hot.shape[1]
    return pl.pallas_call(
        keys_kernel,
        out_shape=(
            jax.ShapeDtypeStruct((SPARE * n, width), BF16),
            jax.ShapeDtypeStruct((n, 2 * width), BF16),
        ),
        in_specs=[VMEM] * 4 + [HBM],
        out_specs=(HBM, VMEM),
        scratch_shapes=[
            pltpu.VMEM((n, width), BF16),
            pltpu.VMEM((n, width), BF16),
            pltpu.VMEM((width, width), BF16),
            pltpu.VMEM((width, width), BF16),
            DMA((4,)),
        ],
        compiler_params=pltpu.CompilerParams(vmem_limit_bytes=KEYS_BYTES),
        cost_estimate=pl.CostEstimate(
            flops=2 * 10**9, bytes_accessed=5 * 10**6, transcendentals=10**6
        ),
        name="keys",
    )(hot, picks, gain, replies, w_in)


def weights(q, k, head_dim):
    half = dot_nt(q, k) * (0.5 / head_dim**0.5)
    return half + half * jnp.tanh(half)


def layer_kernel(
    user, hot, picks, in_gain, gain, replies, other_in, rows_in, own_in, w_in, w_last,
    hist_out, cand_out,
    xs, ins, own, other, w_q, w_u, w_out, qs, us, mix, outs, sems,
):
    n, width = own.shape[0], own.shape[1] // 2
    head_dim = width // HEADS
    hist, cand = pl.ds(0, n), pl.ds(n, n)
    in_q, in_in, in_u, in_own, in_other, in_out, in_x = started(
        (
            (w_in.at[:, pl.ds(2 * width, width)], w_q),
            (rows_in.at[pl.ds(n, n)], ins.at[hist]),
            (w_in.at[:, pl.ds(0, width)], w_u),
            (own_in, own),
            (other_in, other),
            (w_last, w_out),
            (rows_in.at[hist], xs.at[hist]),
        ),
        sems,
    )
    y = picked_cand(replies, hot, to_column(picks[1:2, :]))
    xs[cand, :] = y.astype(BF16)
    ins[cand, :] = norm(y, in_gain[...]).astype(BF16)
    in_q.wait()
    in_in.wait()
    qs[...] = silu(dot(ins[...], w_q[...])).astype(BF16)
    in_u.wait()
    us[...] = silu(dot(ins[...], w_u[...]))
    in_own.wait()
    in_other.wait()
    causal = iota((n, n), 1) <= iota((n, n), 0)

    def heads(everyone):
        for h in range(HEADS):
            at = slice(h * head_dim, (h + 1) * head_dim)
            past = slice(width + h * head_dim, width + (h + 1) * head_dim)
            near = weights(qs[:, at], own[:, at], head_dim)
            near = jnp.concatenate([jnp.where(causal, near[:n], 0.0), near[n:]], axis=0)
            total = dot(near.astype(BF16), own[:, past])
            if everyone:
                far = weights(qs[:, at], other[:, at], head_dim)
                mix[:, at] = total + dot(far.astype(BF16), other[:, past])
            else:
                far = weights(qs[n:, at], other[:, at], head_dim)
                mix[:n, at] = total[:n]
                mix[n:, at] = total[n:] + dot(far.astype(BF16), other[:, past])

    @pl.when(user[0] == 1)
    def _():
        heads(True)

    @pl.when(user[0] == 0)
    def _():
        heads(False)

    in_out.wait()
    in_x.wait()
    done = []
    for i, (rows, out) in enumerate(((hist, hist_out), (cand, cand_out))):
        gated = (norm(mix[rows, :], gain[...]) * us[rows, :]).astype(BF16)
        outs[rows, :] = (xs[rows, :].astype(F32) + dot(gated, w_out[...])).astype(BF16)
        done += started(((outs.at[rows], out),), sems.at[pl.ds(7 + i, 1)])
    for copy in done:
        copy.wait()


def layer(user, replies, hot, picks, in_gain, gain, rows, own, other, w_in, w_out):
    n, width = own.shape[0], own.shape[1] // 2
    shape = jax.ShapeDtypeStruct((n, width), BF16)
    return pl.pallas_call(
        layer_kernel,
        out_shape=(shape, shape),
        in_specs=[SMEM] + [VMEM] * 5 + [HBM] * 5,
        out_specs=(HBM, HBM),
        scratch_shapes=[
            pltpu.VMEM((2 * n, width), BF16),
            pltpu.VMEM((2 * n, width), BF16),
            pltpu.VMEM((n, 2 * width), BF16),
            pltpu.VMEM((n, 2 * width), BF16),
            pltpu.VMEM((width, width), BF16),
            pltpu.VMEM((width, width), BF16),
            pltpu.VMEM((width, width), BF16),
            pltpu.VMEM((2 * n, width), BF16),
            pltpu.VMEM((2 * n, width), F32),
            pltpu.VMEM((2 * n, width), F32),
            pltpu.VMEM((2 * n, width), BF16),
            DMA((9,)),
        ],
        compiler_params=pltpu.CompilerParams(vmem_limit_bytes=LAYER_BYTES),
        cost_estimate=pl.CostEstimate(
            flops=6 * 10**9, bytes_accessed=9 * 10**6, transcendentals=6 * 10**6
        ),
        name="layer",
    )(user, hot, picks, in_gain, gain, replies, other, rows, own, w_in, w_out)


def exchange(array):
    return lax.all_to_all(array, ("req", "cand"), 0, 0, tiled=True)


def per_device(table, hot_table, hot_ids, hist_ids, cand_ids, w_in, w_out, in_gain, attn_gain):
    owners = lax.axis_size("req") * lax.axis_size("cand")
    shift = (table.shape[0] - 1).bit_length()
    asked, picks = ask(hist_ids, cand_ids, hot_ids[None], owners, shift)
    numbers = exchange(asked[:, None, :])[:, 0, :]
    replies = exchange(fetch(numbers, table))
    rows, own = keys(replies, hot_table, picks, w_in[0], in_gain)
    other = lax.ppermute(own, "user", [(0, 1), (1, 0)])
    user = lax.axis_index("user")[None].astype(I32)
    hist_out, cand_out = layer(
        user,
        replies,
        hot_table,
        picks,
        in_gain,
        attn_gain,
        rows,
        own,
        other,
        w_in[0],
        w_out[0],
    )
    return hist_out[None], cand_out[None]


def solution(mesh):
    rows = P(("req", "cand"), None)
    split = P(("req", "cand"), "user")
    in_specs = (rows, P(), P(), split, split, P(), P(), P(), P())
    out_specs = (P(("req", "cand"), "user", None), P(("req", "cand"), "user", None))
    return jax.shard_map(
        per_device, mesh=mesh, in_specs=in_specs, out_specs=out_specs, check_vma=False
    )
```

```python
import jax
import jax.numpy as jnp
from jax import lax
from jax.experimental import pallas as pl
from jax.experimental.pallas import tpu as pltpu
from jax.sharding import PartitionSpec as P

HEADS = 4
SLOTS = 4
LANES = 8
FETCH_PARTS = 2
TABLE_PARTS = 4
SPARE = 16
F32 = jnp.float32
BF16 = jnp.bfloat16
I32 = jnp.int32
ASK_BYTES = 64512 * 1024
VMEM_BYTES = 54528 * 1024
WARM_BYTES = 61440 * 1024
QUERY_BYTES = 52224 * 1024
HBM = pl.BlockSpec(memory_space=pltpu.HBM)
VMEM = pl.BlockSpec(memory_space=pltpu.VMEM)
SMEM = pl.BlockSpec(memory_space=pltpu.SMEM)
KEYS_BYTES = 52224 * 1024
LAYER_BYTES = 51200 * 1024
DMA = pltpu.SemaphoreType.DMA


def iota(shape, dim):
    return lax.broadcasted_iota(I32, shape, dim)


def dot(a, b):
    return jnp.dot(a, b, preferred_element_type=F32)


def dot_nt(a, b):
    return lax.dot_general(a, b, (((1,), (1,)), ((), ())), preferred_element_type=F32)


def to_column(row):
    n = row.shape[1]
    diag = iota((n, n), 0) == iota((n, n), 1)
    return jnp.sum(jnp.where(diag, row, 0.0), axis=1, keepdims=True)


def silu(v):
    half = 0.5 * v
    return half + half * jnp.tanh(half)


def norm(z, gain):
    centred = z - jnp.mean(z, axis=1, keepdims=True)
    variance = jnp.mean(centred * centred, axis=1, keepdims=True)
    return centred * lax.rsqrt(variance + 1e-05) * gain


def started(pairs, sems):
    copies = [pltpu.make_async_copy(a, b, sems.at[i]) for i, (a, b) in enumerate(pairs)]
    for copy in copies:
        copy.start()
    return copies


def ask_kernel(hist_in, cand_in, hot_in, asked, picks, hist_ids, cand_ids, hot_ids, sems, *, owners, shift):
    pairs = ((hot_in, hot_ids), (hist_in, hist_ids), (cand_in, cand_ids))
    for copy in started(pairs, sems):
        copy.wait()
    hot_count = hot_ids.shape[1]
    hot_column = to_column(hot_ids[...].astype(F32))
    total = jnp.zeros((owners, LANES), F32)
    for side, (ids_ref, first) in enumerate(((hist_ids, 0), (cand_ids, SLOTS))):
        ids = ids_ref[...]
        n = ids.shape[1]
        hit = hot_column == ids.astype(F32)
        is_hot = jnp.max(jnp.where(hit, 1.0, 0.0), axis=0, keepdims=True)
        hot_at = jnp.sum(
            jnp.where(hit, iota((hot_count, n), 0).astype(F32), 0.0), axis=0, keepdims=True
        )
        owner = lax.shift_right_logical(ids, shift)
        row = ids & ((1 << shift) - 1)
        of_cold = jnp.where(is_hot > 0.5, -1, owner)
        member = (iota((owners, n), 0) == of_cold).astype(F32)
        member_low = member.astype(BF16)
        earlier = (iota((n, n), 0) < iota((n, n), 1)).astype(F32).astype(BF16)
        before = dot(member_low, earlier)
        rank = jnp.sum(before * member, axis=0, keepdims=True)
        slot = rank + first
        here = iota((LANES, n), 0).astype(F32) == slot
        high = jnp.where(here, lax.shift_right_logical(row, 5).astype(F32), 0.0).astype(BF16)
        low = jnp.where(here, (row & 31).astype(F32), 0.0).astype(BF16)
        total = total + 32.0 * dot_nt(member_low, high) + dot_nt(member_low, low)
        cold_at = owner.astype(F32) * SLOTS + rank
        picks[side : side + 1, :] = jnp.where(is_hot > 0.5, owners * SLOTS + hot_at, cold_at)
    asked[...] = total.astype(I32)


def ask(hist_ids, cand_ids, hot_ids, owners, shift):
    n = hist_ids.shape[1]
    return pl.pallas_call(
        lambda *refs: ask_kernel(*refs, owners=owners, shift=shift),
        out_shape=(
            jax.ShapeDtypeStruct((owners, LANES), I32),
            jax.ShapeDtypeStruct((2, n), F32),
        ),
        in_specs=[HBM] * 3,
        out_specs=(VMEM, VMEM),
        scratch_shapes=[
            pltpu.VMEM((1, n), I32),
            pltpu.VMEM((1, n), I32),
            pltpu.VMEM(hot_ids.shape, I32),
            DMA((3,)),
        ],
        compiler_params=pltpu.CompilerParams(vmem_limit_bytes=ASK_BYTES),
        cost_estimate=pl.CostEstimate(flops=10**9, bytes_accessed=10**5, transcendentals=0),
        name="ask",
    )(hist_ids, cand_ids, hot_ids)


def number_column(numbers, first):
    owners = numbers.shape[0]
    count = owners * SLOTS
    spread = lax.shift_right_logical(iota((count, owners), 0), 2) == iota((count, owners), 1)
    spread = spread.astype(F32).astype(BF16)
    high = lax.shift_right_logical(numbers, 5).astype(F32).astype(BF16)
    low = (numbers & 31).astype(F32).astype(BF16)
    every = 32.0 * dot(spread, high) + dot(spread, low)
    place = iota((count, LANES), 0) & (SLOTS - 1)
    columns = []
    for start in first:
        lane = iota((count, LANES), 1) == place + start
        columns.append(jnp.sum(jnp.where(lane, every, 0.0), axis=1, keepdims=True).astype(I32))
    return columns


def one_hot(column, width):
    hit = iota((column.shape[0], width), 1) == column
    return hit.astype(F32).astype(BF16)


def fetch_kernel(numbers, table_in, out, table, sent, sems):
    owners = numbers.shape[0]
    rows, width = table.shape
    cut = width - width // 4
    piece = rows // TABLE_PARTS
    pieces = [pl.ds(i * piece, piece) for i in range(TABLE_PARTS)]
    arrivals = started(tuple((table_in.at[p], table.at[p]) for p in pieces), sems)
    hist, cand = number_column(numbers[...], (0, SLOTS))
    step = owners // FETCH_PARTS
    count = step * SLOTS
    place = iota((count, step), 0) - (SLOTS - 1) == SLOTS * iota((count, step), 1)
    place = place.astype(F32).astype(BF16)
    last = (iota((count, 1), 0) & (SLOTS - 1)) == SLOTS - 1
    for arrival in arrivals:
        arrival.wait()
    copies = []
    for part in range(FETCH_PARTS):
        mine = slice(part * step, (part + 1) * step)
        block = pl.ds(part * step, step)
        wide = slice(part * count, (part + 1) * count)
        whole = dot(one_hot(hist[wide], rows), table[...])
        sent[mine, :, :width] = whole.reshape(step, SLOTS, width).astype(BF16)
        first = TABLE_PARTS + 2 * part
        side = pl.ds(0, width)
        copies += started(
            ((sent.at[block, :, side], out.at[block, :, side]),), sems.at[pl.ds(first, 1)]
        )
        ends = [
            dot(one_hot(numbers[mine, SLOTS + s : SLOTS + s + 1], rows), table[:, cut:])
            for s in range(SLOTS - 1)
        ]
        ends = jnp.concatenate(ends, axis=1).astype(BF16)
        begin = dot(one_hot(jnp.where(last, -1, cand[wide]), rows), table[:, :cut])
        both = begin + dot(place, ends)
        sent[mine, :, width:] = both.reshape(step, SLOTS, cut).astype(BF16)
        side = pl.ds(width, cut)
        copies += started(
            ((sent.at[block, :, side], out.at[block, :, side]),), sems.at[pl.ds(first + 1, 1)]
        )
    for copy in copies:
        copy.wait()


def fetch(numbers, table):
    owners = numbers.shape[0]
    rows, width = table.shape
    shape = (owners, SLOTS, 2 * width - width // 4)
    return pl.pallas_call(
        fetch_kernel,
        out_shape=jax.ShapeDtypeStruct(shape, BF16),
        in_specs=[VMEM, HBM],
        out_specs=HBM,
        scratch_shapes=[
            pltpu.VMEM(table.shape, BF16),
            pltpu.VMEM(shape, BF16),
            DMA((TABLE_PARTS + 2 * FETCH_PARTS,)),
        ],
        compiler_params=pltpu.CompilerParams(vmem_limit_bytes=VMEM_BYTES),
        cost_estimate=pl.CostEstimate(
            flops=3 * 10**9, bytes_accessed=3 * 10**6, transcendentals=0
        ),
        name="fetch",
    )(numbers, table)


def picked_hist(replies, column, warm):
    owners = replies.shape[0]
    width = warm.shape[1]
    count = owners * SLOTS
    dense = replies[:, :, :width].astype(F32).reshape(count, width).astype(BF16)
    return dot(one_hot(column.astype(I32), count), dense) + warm[...].astype(F32)


def picked_cand(replies, column, warm):
    owners = replies.shape[0]
    width = warm.shape[1]
    count = owners * SLOTS
    part = width // 4
    cut = width - part
    dense = replies[:, :, width:].astype(F32).reshape(count, cut).astype(BF16)
    at = column.astype(I32)
    slot = at & (SLOTS - 1)
    hot = warm[...].astype(F32)
    begin = dot(one_hot(at, count), dense) + hot[:, :cut]
    ends = dot(one_hot(at | (SLOTS - 1), count), dense)
    end = jnp.where(slot == 0, ends[:, :part], ends[:, 2 * part :])
    end = jnp.where(slot == 1, ends[:, part : 2 * part], end)
    end = jnp.where(at < count, end, hot[:, cut:])
    return jnp.concatenate([begin, end], axis=1)


def warm_kernel(picks, hot, out, rows, sems, *, count):
    n = picks.shape[1]
    for side in range(2):
        at = to_column(picks[side : side + 1, :]).astype(I32) - count
        rows[side * n : (side + 1) * n, :] = dot(one_hot(at, hot.shape[0]), hot[...]).astype(BF16)
    (copy,) = started(((rows, out.at[pl.ds(0, 2 * n)]),), sems)
    copy.wait()


def warm_rows(picks, hot, count):
    n = picks.shape[1]
    width = hot.shape[1]
    return pl.pallas_call(
        lambda *refs: warm_kernel(*refs, count=count),
        out_shape=jax.ShapeDtypeStruct((SPARE * n, width), BF16),
        in_specs=[VMEM, VMEM],
        out_specs=HBM,
        scratch_shapes=[pltpu.VMEM((2 * n, width), BF16), DMA((1,))],
        compiler_params=pltpu.CompilerParams(vmem_limit_bytes=WARM_BYTES),
        cost_estimate=pl.CostEstimate(
            flops=10**9, bytes_accessed=2 * 10**6, transcendentals=0
        ),
        name="warm",
    )(picks, hot)


def keys_kernel(
    picks, gain, replies, warm_in, w_in, rows_out, kv, rows, ins, warm, w_v, w_k, sems
):
    n, width = warm.shape[0] // 2, warm.shape[1]
    hist, cand = pl.ds(0, n), pl.ds(n, n)
    in_cand, in_hist, in_v, in_k = started(
        (
            (warm_in.at[cand], warm.at[cand]),
            (warm_in.at[hist], warm.at[hist]),
            (w_in.at[:, pl.ds(width, width)], w_v),
            (w_in.at[:, pl.ds(3 * width, width)], w_k),
        ),
        sems,
    )
    column = to_column(picks[1:2, :])
    in_cand.wait()
    y = picked_cand(replies, column, warm.at[cand])
    rows[cand, :] = y.astype(BF16)
    ins[cand, :] = norm(y, gain[...]).astype(BF16)
    done = started(
        (
            (rows.at[cand], rows_out.at[cand]),
            (ins.at[cand], rows_out.at[pl.ds(3 * n, n)]),
        ),
        sems.at[pl.ds(4, 2)],
    )
    column = to_column(picks[0:1, :])
    in_hist.wait()
    x = picked_hist(replies, column, warm.at[hist])
    rows[hist, :] = x.astype(BF16)
    inner = norm(x, gain[...]).astype(BF16)
    ins[hist, :] = inner
    done += started(
        (
            (rows.at[hist], rows_out.at[hist]),
            (ins.at[hist], rows_out.at[pl.ds(2 * n, n)]),
        ),
        sems.at[pl.ds(6, 2)],
    )
    in_v.wait()
    kv[:, width:] = silu(dot(inner, w_v[...])).astype(BF16)
    in_k.wait()
    kv[:, :width] = silu(dot(inner, w_k[...])).astype(BF16)
    for copy in done:
        copy.wait()


def keys(replies, warm, picks, w_in, gain):
    n = picks.shape[1]
    width = warm.shape[1]
    return pl.pallas_call(
        keys_kernel,
        out_shape=(
            jax.ShapeDtypeStruct((SPARE * n, width), BF16),
            jax.ShapeDtypeStruct((n, 2 * width), BF16),
        ),
        in_specs=[VMEM] * 3 + [HBM] * 2,
        out_specs=(HBM, VMEM),
        scratch_shapes=[
            pltpu.VMEM((2 * n, width), BF16),
            pltpu.VMEM((2 * n, width), BF16),
            pltpu.VMEM((2 * n, width), BF16),
            pltpu.VMEM((width, width), BF16),
            pltpu.VMEM((width, width), BF16),
            DMA((8,)),
        ],
        compiler_params=pltpu.CompilerParams(vmem_limit_bytes=KEYS_BYTES),
        cost_estimate=pl.CostEstimate(
            flops=3 * 10**9, bytes_accessed=6 * 10**6, transcendentals=10**6
        ),
        name="keys",
    )(picks, gain, replies, warm, w_in)


def queries_kernel(rows_in, w_in, u_out, qs, us, ins, w_u, w_q, sems):
    n, width = ins.shape[0] // 2, ins.shape[1]
    hist, cand = pl.ds(0, n), pl.ds(n, n)
    in_hist, in_u, in_cand, in_q = started(
        (
            (rows_in.at[pl.ds(2 * n, n)], ins.at[hist]),
            (w_in.at[:, pl.ds(0, width)], w_u),
            (rows_in.at[pl.ds(3 * n, n)], ins.at[cand]),
            (w_in.at[:, pl.ds(2 * width, width)], w_q),
        ),
        sems,
    )
    in_hist.wait()
    in_u.wait()
    us[hist, :] = silu(dot(ins[hist, :], w_u[...]))
    done = started(((us.at[hist], u_out.at[hist]),), sems.at[pl.ds(4, 1)])
    in_cand.wait()
    us[cand, :] = silu(dot(ins[cand, :], w_u[...]))
    done += started(((us.at[cand], u_out.at[cand]),), sems.at[pl.ds(5, 1)])
    in_q.wait()
    qs[...] = silu(dot(ins[...], w_q[...])).astype(BF16)
    for copy in done:
        copy.wait()


def queries(rows, w_in):
    n, width = rows.shape[0] // SPARE, rows.shape[1]
    return pl.pallas_call(
        queries_kernel,
        out_shape=(
            jax.ShapeDtypeStruct((SPARE * n, width), F32),
            jax.ShapeDtypeStruct((2 * n, width), BF16),
        ),
        in_specs=[HBM, HBM],
        out_specs=(HBM, VMEM),
        scratch_shapes=[
            pltpu.VMEM((2 * n, width), F32),
            pltpu.VMEM((2 * n, width), BF16),
            pltpu.VMEM((width, width), BF16),
            pltpu.VMEM((width, width), BF16),
            DMA((6,)),
        ],
        compiler_params=pltpu.CompilerParams(vmem_limit_bytes=QUERY_BYTES),
        cost_estimate=pl.CostEstimate(
            flops=2 * 10**9, bytes_accessed=4 * 10**6, transcendentals=10**6
        ),
        name="queries",
    )(rows, w_in)


def weights(q, k, head_dim):
    half = dot_nt(q, k) * (0.5 / head_dim**0.5)
    return half + half * jnp.tanh(half)


def layer_kernel(
    user, gain, qs, own, other, rows_in, us_in, w_last, hist_out, cand_out,
    xs, us, w_out, mix, outs, sems,
):
    n, width = own.shape[0], own.shape[1] // 2
    head_dim = width // HEADS
    hist, cand = pl.ds(0, n), pl.ds(n, n)
    both = pl.ds(0, 2 * n)
    arrivals = started(
        ((w_last, w_out), (us_in.at[both], us), (rows_in.at[both], xs)), sems
    )
    causal = iota((n, n), 1) <= iota((n, n), 0)

    def heads(everyone):
        for h in range(HEADS):
            at = slice(h * head_dim, (h + 1) * head_dim)
            past = slice(width + h * head_dim, width + (h + 1) * head_dim)
            near = weights(qs[:, at], own[:, at], head_dim)
            near = jnp.concatenate([jnp.where(causal, near[:n], 0.0), near[n:]], axis=0)
            total = dot(near.astype(BF16), own[:, past])
            if everyone:
                far = weights(qs[:, at], other[:, at], head_dim)
                mix[:, at] = total + dot(far.astype(BF16), other[:, past])
            else:
                far = weights(qs[n:, at], other[:, at], head_dim)
                mix[:n, at] = total[:n]
                mix[n:, at] = total[n:] + dot(far.astype(BF16), other[:, past])

    @pl.when(user[0] == 1)
    def _():
        heads(True)

    @pl.when(user[0] == 0)
    def _():
        heads(False)

    for arrival in arrivals:
        arrival.wait()
    done = []
    for i, (rows, out) in enumerate(((hist, hist_out), (cand, cand_out))):
        gated = (norm(mix[rows, :], gain[...]) * us[rows, :]).astype(BF16)
        outs[rows, :] = (xs[rows, :].astype(F32) + dot(gated, w_out[...])).astype(BF16)
        done += started(((outs.at[rows], out),), sems.at[pl.ds(3 + i, 1)])
    for copy in done:
        copy.wait()


def layer(user, rows, us, qs, own, other, gain, w_out):
    n, width = own.shape[0], own.shape[1] // 2
    shape = jax.ShapeDtypeStruct((n, width), BF16)
    return pl.pallas_call(
        layer_kernel,
        out_shape=(shape, shape),
        in_specs=[SMEM] + [VMEM] * 4 + [HBM] * 3,
        out_specs=(HBM, HBM),
        scratch_shapes=[
            pltpu.VMEM((2 * n, width), BF16),
            pltpu.VMEM((2 * n, width), F32),
            pltpu.VMEM((width, width), BF16),
            pltpu.VMEM((2 * n, width), F32),
            pltpu.VMEM((2 * n, width), BF16),
            DMA((5,)),
        ],
        compiler_params=pltpu.CompilerParams(vmem_limit_bytes=LAYER_BYTES),
        cost_estimate=pl.CostEstimate(
            flops=6 * 10**9, bytes_accessed=9 * 10**6, transcendentals=6 * 10**6
        ),
        name="layer",
    )(user, gain, qs, own, other, rows, us, w_out)


def exchange(array):
    return lax.all_to_all(array, ("req", "cand"), 0, 0, tiled=True)


def per_device(table, hot_table, hot_ids, hist_ids, cand_ids, w_in, w_out, in_gain, attn_gain):
    owners = lax.axis_size("req") * lax.axis_size("cand")
    shift = (table.shape[0] - 1).bit_length()
    asked, picks = ask(hist_ids, cand_ids, hot_ids[None], owners, shift)
    numbers = exchange(asked[:, None, :])[:, 0, :]
    replies = exchange(fetch(numbers, table))
    warm = warm_rows(picks, hot_table, owners * SLOTS)
    rows, own = keys(replies, warm, picks, w_in[0], in_gain)
    other = lax.ppermute(own, "user", [(0, 1), (1, 0)])
    us, qs = queries(rows, w_in[0])
    user = lax.axis_index("user")[None].astype(I32)
    hist_out, cand_out = layer(user, rows, us, qs, own, other, attn_gain, w_out[0])
    return hist_out[None], cand_out[None]


def solution(mesh):
    rows = P(("req", "cand"), None)
    split = P(("req", "cand"), "user")
    in_specs = (rows, P(), P(), split, split, P(), P(), P(), P())
    out_specs = (P(("req", "cand"), "user", None), P(("req", "cand"), "user", None))
    return jax.shard_map(
        per_device, mesh=mesh, in_specs=in_specs, out_specs=out_specs, check_vma=False
    )
```

```python
import jax
import jax.numpy as jnp
from jax import lax
from jax.experimental import pallas as pl
from jax.experimental.pallas import tpu as pltpu
from jax.sharding import PartitionSpec as P

HEADS = 4
SLOTS = 4
LANES = 8
FETCH_PARTS = 2
SPARE = 16
F32 = jnp.float32
BF16 = jnp.bfloat16
I32 = jnp.int32
ASK_BYTES = 53248 * 1024
VMEM_BYTES = 53248 * 1024
WARM_BYTES = 54528 * 1024
QUERY_BYTES = 52224 * 1024
HBM = pl.BlockSpec(memory_space=pltpu.HBM)
VMEM = pl.BlockSpec(memory_space=pltpu.VMEM)
SMEM = pl.BlockSpec(memory_space=pltpu.SMEM)
KEYS_BYTES = 52224 * 1024
LAYER_BYTES = 51200 * 1024
DMA = pltpu.SemaphoreType.DMA


def iota(shape, dim):
    return lax.broadcasted_iota(I32, shape, dim)


def dot(a, b):
    return jnp.dot(a, b, preferred_element_type=F32)


def dot_nt(a, b):
    return lax.dot_general(a, b, (((1,), (1,)), ((), ())), preferred_element_type=F32)


def to_column(row):
    n = row.shape[1]
    diag = iota((n, n), 0) == iota((n, n), 1)
    return jnp.sum(jnp.where(diag, row, 0.0), axis=1, keepdims=True)


def silu(v):
    half = 0.5 * v
    return half + half * jnp.tanh(half)


def norm(z, gain):
    centred = z - jnp.mean(z, axis=1, keepdims=True)
    variance = jnp.mean(centred * centred, axis=1, keepdims=True)
    return centred * lax.rsqrt(variance + 1e-05) * gain


def started(pairs, sems):
    copies = [pltpu.make_async_copy(a, b, sems.at[i]) for i, (a, b) in enumerate(pairs)]
    for copy in copies:
        copy.start()
    return copies


def ask_kernel(ids_in, asked, picks, *, owners, shift):
    n = picks.shape[1]
    hot_count = ids_in.shape[1] - 2 * n
    hot_column = to_column(ids_in[:, 2 * n :].astype(F32))
    total = jnp.zeros((owners, LANES), F32)
    for side, first in enumerate((0, SLOTS)):
        ids = ids_in[:, side * n : (side + 1) * n]
        hit = hot_column == ids.astype(F32)
        is_hot = jnp.max(jnp.where(hit, 1.0, 0.0), axis=0, keepdims=True)
        hot_at = jnp.sum(
            jnp.where(hit, iota((hot_count, n), 0).astype(F32), 0.0), axis=0, keepdims=True
        )
        owner = lax.shift_right_logical(ids, shift)
        row = ids & ((1 << shift) - 1)
        of_cold = jnp.where(is_hot > 0.5, -1, owner)
        member = (iota((owners, n), 0) == of_cold).astype(F32)
        member_low = member.astype(BF16)
        earlier = (iota((n, n), 0) < iota((n, n), 1)).astype(F32).astype(BF16)
        before = dot(member_low, earlier)
        rank = jnp.sum(before * member, axis=0, keepdims=True)
        slot = rank + first
        here = iota((LANES, n), 0).astype(F32) == slot
        high = jnp.where(here, lax.shift_right_logical(row, 5).astype(F32), 0.0).astype(BF16)
        low = jnp.where(here, (row & 31).astype(F32), 0.0).astype(BF16)
        total = total + 32.0 * dot_nt(member_low, high) + dot_nt(member_low, low)
        cold_at = owner.astype(F32) * SLOTS + rank
        picks[side : side + 1, :] = jnp.where(is_hot > 0.5, owners * SLOTS + hot_at, cold_at)
    asked[...] = total.astype(I32)


def ask(hist_ids, cand_ids, hot_ids, owners, shift):
    n = hist_ids.shape[1]
    ids = jnp.concatenate([hist_ids, cand_ids, hot_ids], axis=1)
    return pl.pallas_call(
        lambda *refs: ask_kernel(*refs, owners=owners, shift=shift),
        out_shape=(
            jax.ShapeDtypeStruct((owners, LANES), I32),
            jax.ShapeDtypeStruct((2, n), F32),
        ),
        compiler_params=pltpu.CompilerParams(vmem_limit_bytes=ASK_BYTES),
        cost_estimate=pl.CostEstimate(flops=10**9, bytes_accessed=10**5, transcendentals=0),
        name="ask",
    )(ids)


def number_column(numbers, first):
    owners = numbers.shape[0]
    count = owners * SLOTS
    spread = lax.shift_right_logical(iota((count, owners), 0), 2) == iota((count, owners), 1)
    spread = spread.astype(F32).astype(BF16)
    high = lax.shift_right_logical(numbers, 5).astype(F32).astype(BF16)
    low = (numbers & 31).astype(F32).astype(BF16)
    every = 32.0 * dot(spread, high) + dot(spread, low)
    place = iota((count, LANES), 0) & (SLOTS - 1)
    columns = []
    for start in first:
        lane = iota((count, LANES), 1) == place + start
        columns.append(jnp.sum(jnp.where(lane, every, 0.0), axis=1, keepdims=True).astype(I32))
    return columns


def one_hot(column, width):
    hit = iota((column.shape[0], width), 1) == column
    return hit.astype(F32).astype(BF16)


def moved_down(x, rows):
    return pltpu.roll(x.reshape(x.shape[0] // 8, 8, x.shape[1]), rows, 1).reshape(x.shape)


def fetch_kernel(numbers, table, out, sent, sems):
    owners = numbers.shape[0]
    rows, width = table.shape
    part = width // 4
    cut = width - part
    hist, cand = number_column(numbers[...], (0, SLOTS))
    step = owners // FETCH_PARTS
    count = step * SLOTS
    last = (iota((count, 1), 0) & (SLOTS - 1)) == SLOTS - 1
    copies = []
    for i in range(FETCH_PARTS):
        mine = slice(i * step, (i + 1) * step)
        block = pl.ds(i * step, step)
        wide = slice(i * count, (i + 1) * count)
        whole = dot(one_hot(hist[wide], rows), table[...])
        sent[mine, :, :width] = whole.astype(BF16).reshape(step, SLOTS, width)
        side = pl.ds(0, width)
        copies += started(
            ((sent.at[block, :, side], out.at[block, :, side]),), sems.at[pl.ds(2 * i, 1)]
        )
        whole = dot(one_hot(cand[wide], rows), table[...])
        ends = whole[:, cut:]
        ends = [moved_down(ends, SLOTS - 1 - s) for s in range(SLOTS - 1)]
        both = jnp.where(last, jnp.concatenate(ends, axis=1), whole[:, :cut])
        sent[mine, :, width:] = both.astype(BF16).reshape(step, SLOTS, cut)
        side = pl.ds(width, cut)
        copies += started(
            ((sent.at[block, :, side], out.at[block, :, side]),), sems.at[pl.ds(2 * i + 1, 1)]
        )
    for copy in copies:
        copy.wait()


def fetch(numbers, table):
    owners = numbers.shape[0]
    rows, width = table.shape
    shape = (owners, SLOTS, 2 * width - width // 4)
    return pl.pallas_call(
        fetch_kernel,
        out_shape=jax.ShapeDtypeStruct(shape, BF16),
        in_specs=[VMEM, VMEM],
        out_specs=HBM,
        scratch_shapes=[pltpu.VMEM(shape, BF16), DMA((2 * FETCH_PARTS,))],
        compiler_params=pltpu.CompilerParams(vmem_limit_bytes=VMEM_BYTES),
        cost_estimate=pl.CostEstimate(
            flops=3 * 10**9, bytes_accessed=3 * 10**6, transcendentals=0
        ),
        name="fetch",
    )(numbers, table)


def picked_hist(replies, column, width):
    owners = replies.shape[0]
    count = owners * SLOTS
    dense = replies[:, :, :width].astype(F32).reshape(count, width).astype(BF16)
    return dot(one_hot(column.astype(I32), count), dense)


def picked_cand(replies, column, width):
    owners = replies.shape[0]
    count = owners * SLOTS
    part = width // 4
    dense = replies[:, :, width:].astype(F32).reshape(count, width - part)
    place = iota((count, 1), 0) & (SLOTS - 1)
    end = moved_down(dense[:, :part], 8 - (SLOTS - 1))
    for s in range(1, SLOTS - 1):
        other = moved_down(dense[:, s * part : (s + 1) * part], 8 - (SLOTS - 1 - s))
        end = jnp.where(place == s, other, end)
    dense = jnp.concatenate([dense, end], axis=1).astype(BF16)
    return dot(one_hot(column.astype(I32), count), dense)


def warm_kernel(picks, hot, out, rows, sems, *, count):
    n = picks.shape[1]
    for side in range(2):
        at = to_column(picks[side : side + 1, :]).astype(I32) - count
        rows[side * n : (side + 1) * n, :] = dot(one_hot(at, hot.shape[0]), hot[...]).astype(BF16)
    (copy,) = started(((rows, out.at[pl.ds(0, 2 * n)]),), sems)
    copy.wait()


def warm_rows(picks, hot, count):
    n = picks.shape[1]
    width = hot.shape[1]
    return pl.pallas_call(
        lambda *refs: warm_kernel(*refs, count=count),
        out_shape=jax.ShapeDtypeStruct((SPARE * n, width), BF16),
        in_specs=[VMEM, VMEM],
        out_specs=HBM,
        scratch_shapes=[pltpu.VMEM((2 * n, width), BF16), DMA((1,))],
        compiler_params=pltpu.CompilerParams(vmem_limit_bytes=WARM_BYTES),
        cost_estimate=pl.CostEstimate(
            flops=10**9, bytes_accessed=2 * 10**6, transcendentals=0
        ),
        name="warm",
    )(picks, hot)


def keys_kernel(
    picks, gain, replies, warm_in, w_in, rows_out, kv, warm, rows, ins, w_v, w_k, sems
):
    n, width = warm.shape[0] // 2, warm.shape[1]
    hist, cand = pl.ds(0, n), pl.ds(n, n)
    in_cand, in_hist, in_v, in_k = started(
        (
            (warm_in.at[cand], warm.at[cand]),
            (warm_in.at[hist], warm.at[hist]),
            (w_in.at[:, pl.ds(width, width)], w_v),
            (w_in.at[:, pl.ds(3 * width, width)], w_k),
        ),
        sems,
    )
    column = to_column(picks[1:2, :])
    y = picked_cand(replies, column, width)
    in_cand.wait()
    y = y + warm[cand, :].astype(F32)
    rows[cand, :] = y.astype(BF16)
    ins[cand, :] = norm(y, gain[...]).astype(BF16)
    done = started(
        (
            (rows.at[cand], rows_out.at[cand]),
            (ins.at[cand], rows_out.at[pl.ds(3 * n, n)]),
        ),
        sems.at[pl.ds(4, 2)],
    )
    column = to_column(picks[0:1, :])
    x = picked_hist(replies, column, width)
    in_hist.wait()
    x = x + warm[hist, :].astype(F32)
    rows[hist, :] = x.astype(BF16)
    inner = norm(x, gain[...]).astype(BF16)
    ins[hist, :] = inner
    done += started(
        (
            (rows.at[hist], rows_out.at[hist]),
            (ins.at[hist], rows_out.at[pl.ds(2 * n, n)]),
        ),
        sems.at[pl.ds(6, 2)],
    )
    in_v.wait()
    kv[:, width:] = silu(dot(inner, w_v[...])).astype(BF16)
    in_k.wait()
    kv[:, :width] = silu(dot(inner, w_k[...])).astype(BF16)
    for copy in done:
        copy.wait()


def keys(replies, warm, picks, w_in, gain):
    n = picks.shape[1]
    width = warm.shape[1]
    return pl.pallas_call(
        keys_kernel,
        out_shape=(
            jax.ShapeDtypeStruct((SPARE * n, width), BF16),
            jax.ShapeDtypeStruct((n, 2 * width), BF16),
        ),
        in_specs=[VMEM] * 3 + [HBM] * 2,
        out_specs=(HBM, VMEM),
        scratch_shapes=[
            pltpu.VMEM((2 * n, width), BF16),
            pltpu.VMEM((2 * n, width), BF16),
            pltpu.VMEM((2 * n, width), BF16),
            pltpu.VMEM((width, width), BF16),
            pltpu.VMEM((width, width), BF16),
            DMA((8,)),
        ],
        compiler_params=pltpu.CompilerParams(vmem_limit_bytes=KEYS_BYTES),
        cost_estimate=pl.CostEstimate(
            flops=3 * 10**9, bytes_accessed=6 * 10**6, transcendentals=10**6
        ),
        name="keys",
    )(picks, gain, replies, warm, w_in)


def queries_kernel(rows_in, w_in, qs, ins, w_q, sems):
    n, width = ins.shape[0] // 2, ins.shape[1]
    hist, cand = pl.ds(0, n), pl.ds(n, n)
    in_hist, in_q, in_cand = started(
        (
            (rows_in.at[pl.ds(2 * n, n)], ins.at[hist]),
            (w_in.at[:, pl.ds(2 * width, width)], w_q),
            (rows_in.at[pl.ds(3 * n, n)], ins.at[cand]),
        ),
        sems,
    )
    in_hist.wait()
    in_q.wait()
    qs[hist, :] = silu(dot(ins[hist, :], w_q[...])).astype(BF16)
    in_cand.wait()
    qs[cand, :] = silu(dot(ins[cand, :], w_q[...])).astype(BF16)


def queries(rows, w_in):
    n, width = rows.shape[0] // SPARE, rows.shape[1]
    return pl.pallas_call(
        queries_kernel,
        out_shape=jax.ShapeDtypeStruct((2 * n, width), BF16),
        in_specs=[HBM, HBM],
        out_specs=VMEM,
        scratch_shapes=[
            pltpu.VMEM((2 * n, width), BF16),
            pltpu.VMEM((width, width), BF16),
            DMA((3,)),
        ],
        compiler_params=pltpu.CompilerParams(vmem_limit_bytes=QUERY_BYTES),
        cost_estimate=pl.CostEstimate(
            flops=2 * 10**9, bytes_accessed=4 * 10**6, transcendentals=10**6
        ),
        name="queries",
    )(rows, w_in)


def weights(q, k, head_dim):
    half = dot_nt(q, k) * (0.5 / head_dim**0.5)
    return half + half * jnp.tanh(half)


def layer_kernel(
    user, gain, qs, own, other, rows_in, w_in, w_last, hist_out, cand_out,
    xs, ins, w_u, w_out, us, mix, outs, sems,
):
    n, width = own.shape[0], own.shape[1] // 2
    head_dim = width // HEADS
    hist, cand = pl.ds(0, n), pl.ds(n, n)
    both = pl.ds(0, 2 * n)
    arrivals = started(
        (
            (rows_in.at[pl.ds(2 * n, 2 * n)], ins),
            (w_in.at[:, pl.ds(0, width)], w_u),
            (w_last, w_out),
            (rows_in.at[both], xs),
        ),
        sems,
    )
    causal = iota((n, n), 1) <= iota((n, n), 0)

    def heads(everyone):
        for h in range(HEADS):
            at = slice(h * head_dim, (h + 1) * head_dim)
            past = slice(width + h * head_dim, width + (h + 1) * head_dim)
            near = weights(qs[:, at], own[:, at], head_dim)
            near = jnp.concatenate([jnp.where(causal, near[:n], 0.0), near[n:]], axis=0)
            total = dot(near.astype(BF16), own[:, past])
            if everyone:
                far = weights(qs[:, at], other[:, at], head_dim)
                mix[:, at] = total + dot(far.astype(BF16), other[:, past])
            else:
                far = weights(qs[n:, at], other[:, at], head_dim)
                mix[:n, at] = total[:n]
                mix[n:, at] = total[n:] + dot(far.astype(BF16), other[:, past])

    @pl.when(user[0] == 1)
    def _():
        heads(True)

    @pl.when(user[0] == 0)
    def _():
        heads(False)

    for arrival in arrivals:
        arrival.wait()
    us[...] = silu(dot(ins[...], w_u[...]))
    done = []
    for i, (rows, out) in enumerate(((hist, hist_out), (cand, cand_out))):
        gated = (norm(mix[rows, :], gain[...]) * us[rows, :]).astype(BF16)
        outs[rows, :] = (xs[rows, :].astype(F32) + dot(gated, w_out[...])).astype(BF16)
        done += started(((outs.at[rows], out),), sems.at[pl.ds(4 + i, 1)])
    for copy in done:
        copy.wait()


def layer(user, rows, qs, own, other, gain, w_in, w_out):
    n, width = own.shape[0], own.shape[1] // 2
    shape = jax.ShapeDtypeStruct((n, width), BF16)
    return pl.pallas_call(
        layer_kernel,
        out_shape=(shape, shape),
        in_specs=[SMEM] + [VMEM] * 4 + [HBM] * 3,
        out_specs=(HBM, HBM),
        scratch_shapes=[
            pltpu.VMEM((2 * n, width), BF16),
            pltpu.VMEM((2 * n, width), BF16),
            pltpu.VMEM((width, width), BF16),
            pltpu.VMEM((width, width), BF16),
            pltpu.VMEM((2 * n, width), F32),
            pltpu.VMEM((2 * n, width), F32),
            pltpu.VMEM((2 * n, width), BF16),
            DMA((6,)),
        ],
        compiler_params=pltpu.CompilerParams(vmem_limit_bytes=LAYER_BYTES),
        cost_estimate=pl.CostEstimate(
            flops=6 * 10**9, bytes_accessed=9 * 10**6, transcendentals=6 * 10**6
        ),
        name="layer",
    )(user, gain, qs, own, other, rows, w_in, w_out)


def exchange(array):
    return lax.all_to_all(array, ("req", "cand"), 0, 0, tiled=True)


def per_device(table, hot_table, hot_ids, hist_ids, cand_ids, w_in, w_out, in_gain, attn_gain):
    owners = lax.axis_size("req") * lax.axis_size("cand")
    shift = (table.shape[0] - 1).bit_length()
    asked, picks = ask(hist_ids, cand_ids, hot_ids[None], owners, shift)
    numbers = exchange(asked[:, None, :])[:, 0, :]
    replies = exchange(fetch(numbers, table))
    warm = warm_rows(picks, hot_table, owners * SLOTS)
    rows, own = keys(replies, warm, picks, w_in[0], in_gain)
    other = lax.ppermute(own, "user", [(0, 1), (1, 0)])
    qs = queries(rows, w_in[0])
    user = lax.axis_index("user")[None].astype(I32)
    hist_out, cand_out = layer(user, rows, qs, own, other, attn_gain, w_in[0], w_out[0])
    return hist_out[None], cand_out[None]


def solution(mesh):
    rows = P(("req", "cand"), None)
    split = P(("req", "cand"), "user")
    in_specs = (rows, P(), P(), split, split, P(), P(), P(), P())
    out_specs = (P(("req", "cand"), "user", None), P(("req", "cand"), "user", None))
    return jax.shard_map(
        per_device, mesh=mesh, in_specs=in_specs, out_specs=out_specs, check_vma=False
    )
```

```python
import jax
import jax.numpy as jnp
from jax import lax
from jax.experimental import pallas as pl
from jax.experimental.pallas import tpu as pltpu
from jax.sharding import PartitionSpec as P

HEADS = 4
SLOTS = 4
LANES = 8
FETCH_PARTS = 2
SPARE = 16
FINISH_PARTS = 2
F32 = jnp.float32
BF16 = jnp.bfloat16
I32 = jnp.int32
ASK_BYTES = 53248 * 1024
VMEM_BYTES = 53248 * 1024
QUERY_BYTES = 52224 * 1024
HBM = pl.BlockSpec(memory_space=pltpu.HBM)
VMEM = pl.BlockSpec(memory_space=pltpu.VMEM)
SMEM = pl.BlockSpec(memory_space=pltpu.SMEM)
KEYS_BYTES = 51712 * 1024
LAYER_BYTES = 51200 * 1024
DMA = pltpu.SemaphoreType.DMA


def iota(shape, dim):
    return lax.broadcasted_iota(I32, shape, dim)


def dot(a, b):
    return jnp.dot(a, b, preferred_element_type=F32)


def dot_nt(a, b):
    return lax.dot_general(a, b, (((1,), (1,)), ((), ())), preferred_element_type=F32)


def to_column(row):
    n = row.shape[1]
    diag = iota((n, n), 0) == iota((n, n), 1)
    return jnp.sum(jnp.where(diag, row, 0.0), axis=1, keepdims=True)


def silu(v):
    half = 0.5 * v
    return half + half * jnp.tanh(half)


def norm(z, gain):
    centred = z - jnp.mean(z, axis=1, keepdims=True)
    variance = jnp.mean(centred * centred, axis=1, keepdims=True)
    return centred * lax.rsqrt(variance + 1e-05) * gain


def started(pairs, sems):
    copies = [pltpu.make_async_copy(a, b, sems.at[i]) for i, (a, b) in enumerate(pairs)]
    for copy in copies:
        copy.start()
    return copies


def ask_kernel(ids_in, asked, picks, *, owners, shift):
    n = picks.shape[1]
    hot_count = ids_in.shape[1] - 2 * n
    hot_column = to_column(ids_in[:, 2 * n :].astype(F32))
    total = jnp.zeros((owners, LANES), F32)
    for side, first in enumerate((0, SLOTS)):
        ids = ids_in[:, side * n : (side + 1) * n]
        hit = hot_column == ids.astype(F32)
        is_hot = jnp.max(jnp.where(hit, 1.0, 0.0), axis=0, keepdims=True)
        hot_at = jnp.sum(
            jnp.where(hit, iota((hot_count, n), 0).astype(F32), 0.0), axis=0, keepdims=True
        )
        owner = lax.shift_right_logical(ids, shift)
        row = ids & ((1 << shift) - 1)
        of_cold = jnp.where(is_hot > 0.5, -1, owner)
        member = (iota((owners, n), 0) == of_cold).astype(F32)
        member_low = member.astype(BF16)
        earlier = (iota((n, n), 0) < iota((n, n), 1)).astype(F32).astype(BF16)
        before = dot(member_low, earlier)
        rank = jnp.sum(before * member, axis=0, keepdims=True)
        slot = rank + first
        here = iota((LANES, n), 0).astype(F32) == slot
        high = jnp.where(here, lax.shift_right_logical(row, 5).astype(F32), 0.0).astype(BF16)
        low = jnp.where(here, (row & 31).astype(F32), 0.0).astype(BF16)
        total = total + 32.0 * dot_nt(member_low, high) + dot_nt(member_low, low)
        cold_at = owner.astype(F32) * SLOTS + rank
        picks[side : side + 1, :] = jnp.where(is_hot > 0.5, owners * SLOTS + hot_at, cold_at)
    asked[...] = total.astype(I32)


def ask(hist_ids, cand_ids, hot_ids, owners, shift):
    n = hist_ids.shape[1]
    ids = jnp.concatenate([hist_ids, cand_ids, hot_ids], axis=1)
    return pl.pallas_call(
        lambda *refs: ask_kernel(*refs, owners=owners, shift=shift),
        out_shape=(
            jax.ShapeDtypeStruct((owners, LANES), I32),
            jax.ShapeDtypeStruct((2, n), F32),
        ),
        compiler_params=pltpu.CompilerParams(vmem_limit_bytes=ASK_BYTES),
        cost_estimate=pl.CostEstimate(flops=10**9, bytes_accessed=10**5, transcendentals=0),
        name="ask",
    )(ids)


def number_column(numbers, first):
    owners = numbers.shape[0]
    count = owners * SLOTS
    spread = lax.shift_right_logical(iota((count, owners), 0), 2) == iota((count, owners), 1)
    spread = spread.astype(F32).astype(BF16)
    high = lax.shift_right_logical(numbers, 5).astype(F32).astype(BF16)
    low = (numbers & 31).astype(F32).astype(BF16)
    every = 32.0 * dot(spread, high) + dot(spread, low)
    place = iota((count, LANES), 0) & (SLOTS - 1)
    columns = []
    for start in first:
        lane = iota((count, LANES), 1) == place + start
        columns.append(jnp.sum(jnp.where(lane, every, 0.0), axis=1, keepdims=True).astype(I32))
    return columns


def one_hot(column, width):
    hit = iota((column.shape[0], width), 1) == column
    return hit.astype(F32).astype(BF16)


def moved_down(x, rows):
    return pltpu.roll(x.reshape(x.shape[0] // 8, 8, x.shape[1]), rows, 1).reshape(x.shape)


def fetch_kernel(numbers, table, out, sent, sems):
    owners = numbers.shape[0]
    rows, width = table.shape
    part = width // 4
    cut = width - part
    hist, cand = number_column(numbers[...], (0, SLOTS))
    step = owners // FETCH_PARTS
    count = step * SLOTS
    last = (iota((count, 1), 0) & (SLOTS - 1)) == SLOTS - 1
    copies = []
    for i in range(FETCH_PARTS):
        mine = slice(i * step, (i + 1) * step)
        block = pl.ds(i * step, step)
        wide = slice(i * count, (i + 1) * count)
        whole = dot(one_hot(hist[wide], rows), table[...])
        sent[mine, :, :width] = whole.astype(BF16).reshape(step, SLOTS, width)
        side = pl.ds(0, width)
        copies += started(
            ((sent.at[block, :, side], out.at[block, :, side]),), sems.at[pl.ds(2 * i, 1)]
        )
        whole = dot(one_hot(cand[wide], rows), table[...])
        ends = whole[:, cut:]
        ends = [moved_down(ends, SLOTS - 1 - s) for s in range(SLOTS - 1)]
        both = jnp.where(last, jnp.concatenate(ends, axis=1), whole[:, :cut])
        sent[mine, :, width:] = both.astype(BF16).reshape(step, SLOTS, cut)
        side = pl.ds(width, cut)
        copies += started(
            ((sent.at[block, :, side], out.at[block, :, side]),), sems.at[pl.ds(2 * i + 1, 1)]
        )
    for copy in copies:
        copy.wait()


def fetch(numbers, table):
    owners = numbers.shape[0]
    rows, width = table.shape
    shape = (owners, SLOTS, 2 * width - width // 4)
    return pl.pallas_call(
        fetch_kernel,
        out_shape=jax.ShapeDtypeStruct(shape, BF16),
        in_specs=[VMEM, VMEM],
        out_specs=HBM,
        scratch_shapes=[pltpu.VMEM(shape, BF16), DMA((2 * FETCH_PARTS,))],
        compiler_params=pltpu.CompilerParams(vmem_limit_bytes=VMEM_BYTES),
        cost_estimate=pl.CostEstimate(
            flops=3 * 10**9, bytes_accessed=3 * 10**6, transcendentals=0
        ),
        name="fetch",
    )(numbers, table)


def picked(dense, column, hot):
    at = column.astype(I32)
    count = dense.shape[0]
    cold = dot(one_hot(at, count), dense)
    return cold + dot(one_hot(at - count, hot.shape[0]), hot[...])


def picked_hist(replies, column, hot):
    owners = replies.shape[0]
    width = hot.shape[1]
    count = owners * SLOTS
    dense = replies[:, :, :width].astype(F32).reshape(count, width).astype(BF16)
    return picked(dense, column, hot)


def picked_cand(replies, column, hot):
    owners = replies.shape[0]
    width = hot.shape[1]
    count = owners * SLOTS
    part = width // 4
    dense = replies[:, :, width:].astype(F32).reshape(count, width - part)
    place = iota((count, 1), 0) & (SLOTS - 1)
    end = moved_down(dense[:, :part], 8 - (SLOTS - 1))
    for s in range(1, SLOTS - 1):
        other = moved_down(dense[:, s * part : (s + 1) * part], 8 - (SLOTS - 1 - s))
        end = jnp.where(place == s, other, end)
    dense = jnp.concatenate([dense, end], axis=1).astype(BF16)
    return picked(dense, column, hot)


def keys_kernel(
    picks, gain, hot, replies, w_in, rows_out, kv, rows, ins, w_v, w_k, sems
):
    n, width = rows.shape[0] // 2, rows.shape[1]
    hist, cand = pl.ds(0, n), pl.ds(n, n)
    in_v, in_k = started(
        (
            (w_in.at[:, pl.ds(width, width)], w_v),
            (w_in.at[:, pl.ds(3 * width, width)], w_k),
        ),
        sems,
    )
    column = to_column(picks[1:2, :])
    y = picked_cand(replies, column, hot)
    rows[cand, :] = y.astype(BF16)
    ins[cand, :] = norm(y, gain[...]).astype(BF16)
    done = started(
        (
            (rows.at[cand], rows_out.at[cand]),
            (ins.at[cand], rows_out.at[pl.ds(3 * n, n)]),
        ),
        sems.at[pl.ds(4, 2)],
    )
    column = to_column(picks[0:1, :])
    x = picked_hist(replies, column, hot)
    rows[hist, :] = x.astype(BF16)
    inner = norm(x, gain[...]).astype(BF16)
    ins[hist, :] = inner
    done += started(
        (
            (rows.at[hist], rows_out.at[hist]),
            (ins.at[hist], rows_out.at[pl.ds(2 * n, n)]),
        ),
        sems.at[pl.ds(6, 2)],
    )
    in_v.wait()
    kv[:, width:] = silu(dot(inner, w_v[...])).astype(BF16)
    in_k.wait()
    kv[:, :width] = silu(dot(inner, w_k[...])).astype(BF16)
    for copy in done:
        copy.wait()


def keys(replies, hot, picks, w_in, gain):
    n = picks.shape[1]
    width = hot.shape[1]
    return pl.pallas_call(
        keys_kernel,
        out_shape=(
            jax.ShapeDtypeStruct((SPARE * n, width), BF16),
            jax.ShapeDtypeStruct((n, 2 * width), BF16),
        ),
        in_specs=[VMEM] * 4 + [HBM],
        out_specs=(HBM, VMEM),
        scratch_shapes=[
            pltpu.VMEM((2 * n, width), BF16),
            pltpu.VMEM((2 * n, width), BF16),
            pltpu.VMEM((width, width), BF16),
            pltpu.VMEM((width, width), BF16),
            DMA((8,)),
        ],
        compiler_params=pltpu.CompilerParams(vmem_limit_bytes=KEYS_BYTES),
        cost_estimate=pl.CostEstimate(
            flops=3 * 10**9, bytes_accessed=6 * 10**6, transcendentals=10**6
        ),
        name="keys",
    )(picks, gain, hot, replies, w_in)


def queries_kernel(rows_in, w_in, qs, ins, w_q, sems):
    n, width = ins.shape[0] // 2, ins.shape[1]
    hist, cand = pl.ds(0, n), pl.ds(n, n)
    in_hist, in_q, in_cand = started(
        (
            (rows_in.at[pl.ds(2 * n, n)], ins.at[hist]),
            (w_in.at[:, pl.ds(2 * width, width)], w_q),
            (rows_in.at[pl.ds(3 * n, n)], ins.at[cand]),
        ),
        sems,
    )
    in_hist.wait()
    in_q.wait()
    qs[hist, :] = silu(dot(ins[hist, :], w_q[...])).astype(BF16)
    in_cand.wait()
    qs[cand, :] = silu(dot(ins[cand, :], w_q[...])).astype(BF16)


def queries(rows, w_in):
    n, width = rows.shape[0] // SPARE, rows.shape[1]
    return pl.pallas_call(
        queries_kernel,
        out_shape=jax.ShapeDtypeStruct((2 * n, width), BF16),
        in_specs=[HBM, HBM],
        out_specs=VMEM,
        scratch_shapes=[
            pltpu.VMEM((2 * n, width), BF16),
            pltpu.VMEM((width, width), BF16),
            DMA((3,)),
        ],
        compiler_params=pltpu.CompilerParams(vmem_limit_bytes=QUERY_BYTES),
        cost_estimate=pl.CostEstimate(
            flops=2 * 10**9, bytes_accessed=4 * 10**6, transcendentals=10**6
        ),
        name="queries",
    )(rows, w_in)


def weights(q, k, head_dim):
    half = dot_nt(q, k) * (0.5 / head_dim**0.5)
    return half + half * jnp.tanh(half)


def layer_kernel(
    user, gain, qs, own, other, rows_in, w_in, w_last, hist_out, cand_out,
    xs, ins, w_u, w_out, us, mix, outs, sems,
):
    n, width = own.shape[0], own.shape[1] // 2
    head_dim = width // HEADS
    hist, cand = pl.ds(0, n), pl.ds(n, n)
    both = pl.ds(0, 2 * n)
    arrivals = started(
        (
            (rows_in.at[pl.ds(2 * n, 2 * n)], ins),
            (w_in.at[:, pl.ds(0, width)], w_u),
            (w_last, w_out),
            (rows_in.at[both], xs),
        ),
        sems,
    )
    half = n // 2
    causal = iota((half, half), 1) <= iota((half, half), 0)

    def masked(w):
        w = jnp.concatenate([jnp.where(causal, w[:half], 0.0), w[half:]], axis=0)
        return w.astype(BF16)

    def heads(everyone):
        for h in range(HEADS):
            at = slice(h * head_dim, (h + 1) * head_dim)
            past = slice(width + h * head_dim, width + (h + 1) * head_dim)
            first = masked(weights(qs[:, at], own[:half, at], head_dim))
            first = dot(first, own[:half, past])
            second = masked(weights(qs[half:, at], own[half:, at], head_dim))
            second = dot(second, own[half:, past])
            if everyone:
                far = weights(qs[:, at], other[:, at], head_dim).astype(BF16)
                far = dot(far, other[:, past])
                mix[:half, at] = first[:half] + far[:half]
                mix[half:, at] = first[half:] + second + far[half:]
            else:
                far = weights(qs[n:, at], other[:, at], head_dim).astype(BF16)
                far = dot(far, other[:, past])
                mix[:half, at] = first[:half]
                mix[half:n, at] = first[half:n] + second[: n - half]
                mix[n:, at] = first[n:] + second[n - half :] + far

    @pl.when(user[0] == 1)
    def _():
        heads(True)

    @pl.when(user[0] == 0)
    def _():
        heads(False)

    for arrival in arrivals:
        arrival.wait()
    us[...] = silu(dot(ins[...], w_u[...]))
    done = []
    step = n // FINISH_PARTS
    for i in range(2 * FINISH_PARTS):
        rows = pl.ds(i * step, step)
        out = hist_out if i < FINISH_PARTS else cand_out
        gated = (norm(mix[rows, :], gain[...]) * us[rows, :]).astype(BF16)
        outs[rows, :] = (xs[rows, :].astype(F32) + dot(gated, w_out[...])).astype(BF16)
        place = pl.ds(i % FINISH_PARTS * step, step)
        done += started(((outs.at[rows], out.at[place]),), sems.at[pl.ds(4 + i, 1)])
    for copy in done:
        copy.wait()


def layer(user, rows, qs, own, other, gain, w_in, w_out):
    n, width = own.shape[0], own.shape[1] // 2
    shape = jax.ShapeDtypeStruct((n, width), BF16)
    return pl.pallas_call(
        layer_kernel,
        out_shape=(shape, shape),
        in_specs=[SMEM] + [VMEM] * 4 + [HBM] * 3,
        out_specs=(HBM, HBM),
        scratch_shapes=[
            pltpu.VMEM((2 * n, width), BF16),
            pltpu.VMEM((2 * n, width), BF16),
            pltpu.VMEM((width, width), BF16),
            pltpu.VMEM((width, width), BF16),
            pltpu.VMEM((2 * n, width), F32),
            pltpu.VMEM((2 * n, width), F32),
            pltpu.VMEM((2 * n, width), BF16),
            DMA((4 + 2 * FINISH_PARTS,)),
        ],
        compiler_params=pltpu.CompilerParams(vmem_limit_bytes=LAYER_BYTES),
        cost_estimate=pl.CostEstimate(
            flops=6 * 10**9, bytes_accessed=9 * 10**6, transcendentals=6 * 10**6
        ),
        name="layer",
    )(user, gain, qs, own, other, rows, w_in, w_out)


def exchange(array):
    return lax.all_to_all(array, ("req", "cand"), 0, 0, tiled=True)


def per_device(table, hot_table, hot_ids, hist_ids, cand_ids, w_in, w_out, in_gain, attn_gain):
    owners = lax.axis_size("req") * lax.axis_size("cand")
    shift = (table.shape[0] - 1).bit_length()
    asked, picks = ask(hist_ids, cand_ids, hot_ids[None], owners, shift)
    numbers = exchange(asked[:, None, :])[:, 0, :]
    replies = exchange(fetch(numbers, table))
    rows, own = keys(replies, hot_table, picks, w_in[0], in_gain)
    other = lax.ppermute(own, "user", [(0, 1), (1, 0)])
    qs = queries(rows, w_in[0])
    user = lax.axis_index("user")[None].astype(I32)
    hist_out, cand_out = layer(user, rows, qs, own, other, attn_gain, w_in[0], w_out[0])
    return hist_out[None], cand_out[None]


def solution(mesh):
    rows = P(("req", "cand"), None)
    split = P(("req", "cand"), "user")
    in_specs = (rows, P(), P(), split, split, P(), P(), P(), P())
    out_specs = (P(("req", "cand"), "user", None), P(("req", "cand"), "user", None))
    return jax.shard_map(
        per_device, mesh=mesh, in_specs=in_specs, out_specs=out_specs, check_vma=False
    )
```

```python
import jax
import jax.numpy as jnp
from jax import lax
from jax.experimental import pallas as pl
from jax.experimental.pallas import tpu as pltpu
from jax.sharding import PartitionSpec as P

HEADS = 4
SLOTS = 4
LANES = 8
FETCH_PARTS = 2
SPARE = 16
FINISH_PARTS = 2
F32 = jnp.float32
BF16 = jnp.bfloat16
I32 = jnp.int32
ASK_BYTES = 53248 * 1024
VMEM_BYTES = 53248 * 1024
QUERY_BYTES = 52224 * 1024
HBM = pl.BlockSpec(memory_space=pltpu.HBM)
VMEM = pl.BlockSpec(memory_space=pltpu.VMEM)
SMEM = pl.BlockSpec(memory_space=pltpu.SMEM)
KEYS_BYTES = 51712 * 1024
LAYER_BYTES = 51200 * 1024
DMA = pltpu.SemaphoreType.DMA


def iota(shape, dim):
    return lax.broadcasted_iota(I32, shape, dim)


def dot(a, b):
    return jnp.dot(a, b, preferred_element_type=F32)


def dot_nt(a, b):
    return lax.dot_general(a, b, (((1,), (1,)), ((), ())), preferred_element_type=F32)


def to_column(row):
    n = row.shape[1]
    diag = iota((n, n), 0) == iota((n, n), 1)
    return jnp.sum(jnp.where(diag, row, 0.0), axis=1, keepdims=True)


def silu(v):
    half = 0.5 * v
    return half + half * jnp.tanh(half)


def norm(z, gain):
    centred = z - jnp.mean(z, axis=1, keepdims=True)
    variance = jnp.mean(centred * centred, axis=1, keepdims=True)
    return centred * lax.rsqrt(variance + 1e-05) * gain


def started(pairs, sems):
    copies = [pltpu.make_async_copy(a, b, sems.at[i]) for i, (a, b) in enumerate(pairs)]
    for copy in copies:
        copy.start()
    return copies


def ask_kernel(ids_in, asked, picks, *, owners, shift):
    n = picks.shape[1]
    hot_count = ids_in.shape[1] - 2 * n
    hot_column = to_column(ids_in[:, 2 * n :].astype(F32))
    total = jnp.zeros((owners, LANES), F32)
    for side, first in enumerate((0, SLOTS)):
        ids = ids_in[:, side * n : (side + 1) * n]
        hit = hot_column == ids.astype(F32)
        is_hot = jnp.max(jnp.where(hit, 1.0, 0.0), axis=0, keepdims=True)
        hot_at = jnp.sum(
            jnp.where(hit, iota((hot_count, n), 0).astype(F32), 0.0), axis=0, keepdims=True
        )
        owner = lax.shift_right_logical(ids, shift)
        row = ids & ((1 << shift) - 1)
        of_cold = jnp.where(is_hot > 0.5, -1, owner)
        member = (iota((owners, n), 0) == of_cold).astype(F32)
        member_low = member.astype(BF16)
        earlier = (iota((n, n), 0) < iota((n, n), 1)).astype(F32).astype(BF16)
        before = dot(member_low, earlier)
        rank = jnp.sum(before * member, axis=0, keepdims=True)
        slot = rank + first
        here = iota((LANES, n), 0).astype(F32) == slot
        high = jnp.where(here, lax.shift_right_logical(row, 5).astype(F32), 0.0).astype(BF16)
        low = jnp.where(here, (row & 31).astype(F32), 0.0).astype(BF16)
        total = total + 32.0 * dot_nt(member_low, high) + dot_nt(member_low, low)
        cold_at = owner.astype(F32) * SLOTS + rank
        picks[side : side + 1, :] = jnp.where(is_hot > 0.5, owners * SLOTS + hot_at, cold_at)
    asked[...] = total.astype(I32)


def ask(hist_ids, cand_ids, hot_ids, owners, shift):
    n = hist_ids.shape[1]
    ids = jnp.concatenate([hist_ids, cand_ids, hot_ids], axis=1)
    return pl.pallas_call(
        lambda *refs: ask_kernel(*refs, owners=owners, shift=shift),
        out_shape=(
            jax.ShapeDtypeStruct((owners, LANES), I32),
            jax.ShapeDtypeStruct((2, n), F32),
        ),
        compiler_params=pltpu.CompilerParams(vmem_limit_bytes=ASK_BYTES),
        cost_estimate=pl.CostEstimate(flops=10**9, bytes_accessed=10**5, transcendentals=0),
        name="ask",
    )(ids)


def number_column(numbers, first):
    owners = numbers.shape[0]
    count = owners * SLOTS
    spread = lax.shift_right_logical(iota((count, owners), 0), 2) == iota((count, owners), 1)
    spread = spread.astype(F32).astype(BF16)
    high = lax.shift_right_logical(numbers, 5).astype(F32).astype(BF16)
    low = (numbers & 31).astype(F32).astype(BF16)
    every = 32.0 * dot(spread, high) + dot(spread, low)
    place = iota((count, LANES), 0) & (SLOTS - 1)
    columns = []
    for start in first:
        lane = iota((count, LANES), 1) == place + start
        columns.append(jnp.sum(jnp.where(lane, every, 0.0), axis=1, keepdims=True).astype(I32))
    return columns


def one_hot(column, width):
    hit = iota((column.shape[0], width), 1) == column
    return hit.astype(F32).astype(BF16)


def moved_down(x, rows):
    return pltpu.roll(x.reshape(x.shape[0] // 8, 8, x.shape[1]), rows, 1).reshape(x.shape)


def fetch_kernel(numbers, table, out, sent, sems):
    owners = numbers.shape[0]
    rows, width = table.shape
    part = width // 4
    cut = width - part
    hist, cand = number_column(numbers[...], (0, SLOTS))
    step = owners // FETCH_PARTS
    count = step * SLOTS
    last = (iota((count, 1), 0) & (SLOTS - 1)) == SLOTS - 1
    copies = []
    for i in range(FETCH_PARTS):
        mine = slice(i * step, (i + 1) * step)
        block = pl.ds(i * step, step)
        wide = slice(i * count, (i + 1) * count)
        whole = dot(one_hot(hist[wide], rows), table[...])
        sent[mine, :, :width] = whole.astype(BF16).reshape(step, SLOTS, width)
        side = pl.ds(0, width)
        copies += started(
            ((sent.at[block, :, side], out.at[block, :, side]),), sems.at[pl.ds(2 * i, 1)]
        )
        whole = dot(one_hot(cand[wide], rows), table[...])
        ends = whole[:, cut:]
        ends = [moved_down(ends, SLOTS - 1 - s) for s in range(SLOTS - 1)]
        both = jnp.where(last, jnp.concatenate(ends, axis=1), whole[:, :cut])
        sent[mine, :, width:] = both.astype(BF16).reshape(step, SLOTS, cut)
        side = pl.ds(width, cut)
        copies += started(
            ((sent.at[block, :, side], out.at[block, :, side]),), sems.at[pl.ds(2 * i + 1, 1)]
        )
    for copy in copies:
        copy.wait()


def fetch(numbers, table):
    owners = numbers.shape[0]
    rows, width = table.shape
    shape = (owners, SLOTS, 2 * width - width // 4)
    return pl.pallas_call(
        fetch_kernel,
        out_shape=jax.ShapeDtypeStruct(shape, BF16),
        in_specs=[VMEM, VMEM],
        out_specs=HBM,
        scratch_shapes=[pltpu.VMEM(shape, BF16), DMA((2 * FETCH_PARTS,))],
        compiler_params=pltpu.CompilerParams(vmem_limit_bytes=VMEM_BYTES),
        cost_estimate=pl.CostEstimate(
            flops=3 * 10**9, bytes_accessed=3 * 10**6, transcendentals=0
        ),
        name="fetch",
    )(numbers, table)


def picked(dense, column, hot):
    at = column.astype(I32)
    count = dense.shape[0]
    cold = dot(one_hot(at, count), dense)
    return cold + dot(one_hot(at - count, hot.shape[0]), hot[...])


def picked_hist(replies, column, hot):
    owners = replies.shape[0]
    width = hot.shape[1]
    count = owners * SLOTS
    dense = replies[:, :, :width].astype(F32).reshape(count, width).astype(BF16)
    return picked(dense, column, hot)


def picked_cand(replies, column, hot):
    owners = replies.shape[0]
    width = hot.shape[1]
    count = owners * SLOTS
    part = width // 4
    dense = replies[:, :, width:].astype(F32).reshape(count, width - part)
    place = iota((count, 1), 0) & (SLOTS - 1)
    end = moved_down(dense[:, :part], 8 - (SLOTS - 1))
    for s in range(1, SLOTS - 1):
        other = moved_down(dense[:, s * part : (s + 1) * part], 8 - (SLOTS - 1 - s))
        end = jnp.where(place == s, other, end)
    dense = jnp.concatenate([dense, end], axis=1).astype(BF16)
    return picked(dense, column, hot)


def weights(q, k, head_dim):
    half = dot_nt(q, k) * (0.5 / head_dim**0.5)
    return half + half * jnp.tanh(half)


def causal_parts(q, kv, half, at, past, head_dim):
    causal = iota((half, half), 1) <= iota((half, half), 0)

    def masked(w):
        top = jnp.where(causal, w[:half], 0.0)
        if w.shape[0] > half:
            top = jnp.concatenate([top, w[half:]], axis=0)
        return top.astype(BF16)

    first = masked(weights(q[:, at], kv[:half, at], head_dim))
    second = masked(weights(q[half:, at], kv[half:, at], head_dim))
    return dot(first, kv[:half, past]), dot(second, kv[half:, past])


def keys_kernel(
    user, picks, gain, hot, replies, w_in, rows_out, near_out, kv,
    rows, ins, w_v, w_k, w_q, near, sems,
):
    n, width = rows.shape[0] // 2, rows.shape[1]
    hist, cand = pl.ds(0, n), pl.ds(n, n)
    in_v, in_k, in_q = started(
        (
            (w_in.at[:, pl.ds(width, width)], w_v),
            (w_in.at[:, pl.ds(3 * width, width)], w_k),
            (w_in.at[:, pl.ds(2 * width, width)], w_q),
        ),
        sems,
    )
    column = to_column(picks[1:2, :])
    y = picked_cand(replies, column, hot)
    rows[cand, :] = y.astype(BF16)
    ins[cand, :] = norm(y, gain[...]).astype(BF16)
    done = started(
        (
            (rows.at[cand], rows_out.at[cand]),
            (ins.at[cand], rows_out.at[pl.ds(3 * n, n)]),
        ),
        sems.at[pl.ds(4, 2)],
    )
    column = to_column(picks[0:1, :])
    x = picked_hist(replies, column, hot)
    rows[hist, :] = x.astype(BF16)
    inner = norm(x, gain[...]).astype(BF16)
    ins[hist, :] = inner
    done += started(
        (
            (rows.at[hist], rows_out.at[hist]),
            (ins.at[hist], rows_out.at[pl.ds(2 * n, n)]),
        ),
        sems.at[pl.ds(6, 2)],
    )
    in_v.wait()
    kv[:, width:] = silu(dot(inner, w_v[...])).astype(BF16)
    in_k.wait()
    kv[:, :width] = silu(dot(inner, w_k[...])).astype(BF16)
    in_q.wait()

    @pl.when(user[0] == 1)
    def _():
        q = silu(dot(ins[hist, :], w_q[...])).astype(BF16)
        half = n // 2
        head_dim = width // HEADS
        for h in range(HEADS):
            at = slice(h * head_dim, (h + 1) * head_dim)
            past = slice(width + h * head_dim, width + (h + 1) * head_dim)
            first, second = causal_parts(q, kv, half, at, past, head_dim)
            near[:half, at] = first[:half]
            near[half:, at] = first[half:] + second
        (copy,) = started(((near, near_out.at[hist]),), sems.at[pl.ds(8, 1)])
        copy.wait()

    for copy in done:
        copy.wait()


def keys(user, replies, hot, picks, w_in, gain):
    n = picks.shape[1]
    width = hot.shape[1]
    return pl.pallas_call(
        keys_kernel,
        out_shape=(
            jax.ShapeDtypeStruct((SPARE * n, width), BF16),
            jax.ShapeDtypeStruct((SPARE // 2 * n, width), F32),
            jax.ShapeDtypeStruct((n, 2 * width), BF16),
        ),
        in_specs=[SMEM] + [VMEM] * 4 + [HBM],
        out_specs=(HBM, HBM, VMEM),
        scratch_shapes=[
            pltpu.VMEM((2 * n, width), BF16),
            pltpu.VMEM((2 * n, width), BF16),
            pltpu.VMEM((width, width), BF16),
            pltpu.VMEM((width, width), BF16),
            pltpu.VMEM((width, width), BF16),
            pltpu.VMEM((n, width), F32),
            DMA((9,)),
        ],
        compiler_params=pltpu.CompilerParams(vmem_limit_bytes=KEYS_BYTES),
        cost_estimate=pl.CostEstimate(
            flops=3 * 10**9, bytes_accessed=6 * 10**6, transcendentals=10**6
        ),
        name="keys",
    )(user, picks, gain, hot, replies, w_in)


def queries_kernel(rows_in, w_in, qs, ins, w_q, sems):
    n, width = ins.shape[0] // 2, ins.shape[1]
    hist, cand = pl.ds(0, n), pl.ds(n, n)
    in_hist, in_q, in_cand = started(
        (
            (rows_in.at[pl.ds(2 * n, n)], ins.at[hist]),
            (w_in.at[:, pl.ds(2 * width, width)], w_q),
            (rows_in.at[pl.ds(3 * n, n)], ins.at[cand]),
        ),
        sems,
    )
    in_hist.wait()
    in_q.wait()
    qs[hist, :] = silu(dot(ins[hist, :], w_q[...])).astype(BF16)
    in_cand.wait()
    qs[cand, :] = silu(dot(ins[cand, :], w_q[...])).astype(BF16)


def queries(rows, w_in):
    n, width = rows.shape[0] // SPARE, rows.shape[1]
    return pl.pallas_call(
        queries_kernel,
        out_shape=jax.ShapeDtypeStruct((2 * n, width), BF16),
        in_specs=[HBM, HBM],
        out_specs=VMEM,
        scratch_shapes=[
            pltpu.VMEM((2 * n, width), BF16),
            pltpu.VMEM((width, width), BF16),
            DMA((3,)),
        ],
        compiler_params=pltpu.CompilerParams(vmem_limit_bytes=QUERY_BYTES),
        cost_estimate=pl.CostEstimate(
            flops=2 * 10**9, bytes_accessed=4 * 10**6, transcendentals=10**6
        ),
        name="queries",
    )(rows, w_in)


def layer_kernel(
    user, gain, qs, own, other, rows_in, near_in, w_in, w_last, hist_out, cand_out,
    xs, ins, near, w_u, w_out, us, mix, outs, sems,
):
    n, width = own.shape[0], own.shape[1] // 2
    head_dim = width // HEADS
    hist, cand = pl.ds(0, n), pl.ds(n, n)
    both = pl.ds(0, 2 * n)
    arrivals = started(
        (
            (rows_in.at[pl.ds(2 * n, 2 * n)], ins),
            (w_in.at[:, pl.ds(0, width)], w_u),
            (w_last, w_out),
            (rows_in.at[both], xs),
        ),
        sems,
    )
    half = n // 2

    @pl.when(user[0] == 1)
    def _():
        last = 4 + 2 * FINISH_PARTS
        (copy,) = started(((near_in.at[hist], near),), sems.at[pl.ds(last, 1)])
        for h in range(HEADS):
            at = slice(h * head_dim, (h + 1) * head_dim)
            past = slice(width + h * head_dim, width + (h + 1) * head_dim)
            first = weights(qs[n:, at], own[:, at], head_dim).astype(BF16)
            first = dot(first, own[:, past])
            far = weights(qs[:, at], other[:, at], head_dim).astype(BF16)
            far = dot(far, other[:, past])
            mix[:n, at] = far[:n]
            mix[n:, at] = first + far[n:]
        copy.wait()
        mix[:n, :] += near[...]

    @pl.when(user[0] == 0)
    def _():
        for h in range(HEADS):
            at = slice(h * head_dim, (h + 1) * head_dim)
            past = slice(width + h * head_dim, width + (h + 1) * head_dim)
            first, second = causal_parts(qs, own, half, at, past, head_dim)
            far = weights(qs[n:, at], other[:, at], head_dim).astype(BF16)
            far = dot(far, other[:, past])
            mix[:half, at] = first[:half]
            mix[half:n, at] = first[half:n] + second[: n - half]
            mix[n:, at] = first[n:] + second[n - half :] + far

    for arrival in arrivals:
        arrival.wait()
    us[...] = silu(dot(ins[...], w_u[...]))
    done = []
    step = n // FINISH_PARTS
    for i in range(2 * FINISH_PARTS):
        rows = pl.ds(i * step, step)
        out = hist_out if i < FINISH_PARTS else cand_out
        gated = (norm(mix[rows, :], gain[...]) * us[rows, :]).astype(BF16)
        outs[rows, :] = (xs[rows, :].astype(F32) + dot(gated, w_out[...])).astype(BF16)
        place = pl.ds(i % FINISH_PARTS * step, step)
        done += started(((outs.at[rows], out.at[place]),), sems.at[pl.ds(4 + i, 1)])
    for copy in done:
        copy.wait()


def layer(user, rows, near, qs, own, other, gain, w_in, w_out):
    n, width = own.shape[0], own.shape[1] // 2
    shape = jax.ShapeDtypeStruct((n, width), BF16)
    return pl.pallas_call(
        layer_kernel,
        out_shape=(shape, shape),
        in_specs=[SMEM] + [VMEM] * 4 + [HBM] * 4,
        out_specs=(HBM, HBM),
        scratch_shapes=[
            pltpu.VMEM((2 * n, width), BF16),
            pltpu.VMEM((2 * n, width), BF16),
            pltpu.VMEM((n, width), F32),
            pltpu.VMEM((width, width), BF16),
            pltpu.VMEM((width, width), BF16),
            pltpu.VMEM((2 * n, width), F32),
            pltpu.VMEM((2 * n, width), F32),
            pltpu.VMEM((2 * n, width), BF16),
            DMA((5 + 2 * FINISH_PARTS,)),
        ],
        compiler_params=pltpu.CompilerParams(vmem_limit_bytes=LAYER_BYTES),
        cost_estimate=pl.CostEstimate(
            flops=6 * 10**9, bytes_accessed=9 * 10**6, transcendentals=6 * 10**6
        ),
        name="layer",
    )(user, gain, qs, own, other, rows, near, w_in, w_out)


def exchange(array):
    return lax.all_to_all(array, ("req", "cand"), 0, 0, tiled=True)


def per_device(table, hot_table, hot_ids, hist_ids, cand_ids, w_in, w_out, in_gain, attn_gain):
    owners = lax.axis_size("req") * lax.axis_size("cand")
    shift = (table.shape[0] - 1).bit_length()
    asked, picks = ask(hist_ids, cand_ids, hot_ids[None], owners, shift)
    numbers = exchange(asked[:, None, :])[:, 0, :]
    replies = exchange(fetch(numbers, table))
    user = lax.axis_index("user")[None].astype(I32)
    rows, near, own = keys(user, replies, hot_table, picks, w_in[0], in_gain)
    other = lax.ppermute(own, "user", [(0, 1), (1, 0)])
    qs = queries(rows, w_in[0])
    hist_out, cand_out = layer(user, rows, near, qs, own, other, attn_gain, w_in[0], w_out[0])
    return hist_out[None], cand_out[None]


def solution(mesh):
    rows = P(("req", "cand"), None)
    split = P(("req", "cand"), "user")
    in_specs = (rows, P(), P(), split, split, P(), P(), P(), P())
    out_specs = (P(("req", "cand"), "user", None), P(("req", "cand"), "user", None))
    return jax.shard_map(
        per_device, mesh=mesh, in_specs=in_specs, out_specs=out_specs, check_vma=False
    )
```

```python
import jax
import jax.numpy as jnp
from jax import lax
from jax.experimental import pallas as pl
from jax.experimental.pallas import tpu as pltpu
from jax.sharding import PartitionSpec as P

HEADS = 4
SLOTS = 4
LANES = 8
FETCH_PARTS = 2
SPARE = 16
FINISH_PARTS = 2
F32 = jnp.float32
BF16 = jnp.bfloat16
I32 = jnp.int32
ASK_BYTES = 53248 * 1024
VMEM_BYTES = 53248 * 1024
QUERY_BYTES = 52224 * 1024
HBM = pl.BlockSpec(memory_space=pltpu.HBM)
VMEM = pl.BlockSpec(memory_space=pltpu.VMEM)
SMEM = pl.BlockSpec(memory_space=pltpu.SMEM)
KEYS_BYTES = 51712 * 1024
LAYER_BYTES = 51200 * 1024
DMA = pltpu.SemaphoreType.DMA


def iota(shape, dim):
    return lax.broadcasted_iota(I32, shape, dim)


def dot(a, b):
    return jnp.dot(a, b, preferred_element_type=F32)


def dot_nt(a, b):
    return lax.dot_general(a, b, (((1,), (1,)), ((), ())), preferred_element_type=F32)


def to_column(row):
    n = row.shape[1]
    diag = iota((n, n), 0) == iota((n, n), 1)
    return jnp.sum(jnp.where(diag, row, 0.0), axis=1, keepdims=True)


def silu(v):
    half = 0.5 * v
    return half + half * jnp.tanh(half)


def norm(z, gain):
    centred = z - jnp.mean(z, axis=1, keepdims=True)
    variance = jnp.mean(centred * centred, axis=1, keepdims=True)
    return centred * lax.rsqrt(variance + 1e-05) * gain


def started(pairs, sems):
    copies = [pltpu.make_async_copy(a, b, sems.at[i]) for i, (a, b) in enumerate(pairs)]
    for copy in copies:
        copy.start()
    return copies


def ask_kernel(ids_in, asked, picks, *, owners, shift):
    n = picks.shape[1]
    hot_count = ids_in.shape[1] - 2 * n
    hot_column = to_column(ids_in[:, 2 * n :].astype(F32))
    total = jnp.zeros((owners, LANES), F32)
    for side, first in enumerate((0, SLOTS)):
        ids = ids_in[:, side * n : (side + 1) * n]
        hit = hot_column == ids.astype(F32)
        is_hot = jnp.max(jnp.where(hit, 1.0, 0.0), axis=0, keepdims=True)
        hot_at = jnp.sum(
            jnp.where(hit, iota((hot_count, n), 0).astype(F32), 0.0), axis=0, keepdims=True
        )
        owner = lax.shift_right_logical(ids, shift)
        row = ids & ((1 << shift) - 1)
        of_cold = jnp.where(is_hot > 0.5, -1, owner)
        member = (iota((owners, n), 0) == of_cold).astype(F32)
        member_low = member.astype(BF16)
        earlier = (iota((n, n), 0) < iota((n, n), 1)).astype(F32).astype(BF16)
        before = dot(member_low, earlier)
        rank = jnp.sum(before * member, axis=0, keepdims=True)
        slot = rank + first
        here = iota((LANES, n), 0).astype(F32) == slot
        high = jnp.where(here, lax.shift_right_logical(row, 5).astype(F32), 0.0).astype(BF16)
        low = jnp.where(here, (row & 31).astype(F32), 0.0).astype(BF16)
        total = total + 32.0 * dot_nt(member_low, high) + dot_nt(member_low, low)
        cold_at = owner.astype(F32) * SLOTS + rank
        picks[side : side + 1, :] = jnp.where(is_hot > 0.5, owners * SLOTS + hot_at, cold_at)
    asked[...] = total.astype(I32)


def ask(hist_ids, cand_ids, hot_ids, owners, shift):
    n = hist_ids.shape[1]
    ids = jnp.concatenate([hist_ids, cand_ids, hot_ids], axis=1)
    return pl.pallas_call(
        lambda *refs: ask_kernel(*refs, owners=owners, shift=shift),
        out_shape=(
            jax.ShapeDtypeStruct((owners, LANES), I32),
            jax.ShapeDtypeStruct((2, n), F32),
        ),
        compiler_params=pltpu.CompilerParams(vmem_limit_bytes=ASK_BYTES),
        cost_estimate=pl.CostEstimate(flops=10**9, bytes_accessed=10**5, transcendentals=0),
        name="ask",
    )(ids)


def number_column(numbers, first):
    owners = numbers.shape[0]
    count = owners * SLOTS
    spread = lax.shift_right_logical(iota((count, owners), 0), 2) == iota((count, owners), 1)
    spread = spread.astype(F32).astype(BF16)
    high = lax.shift_right_logical(numbers, 5).astype(F32).astype(BF16)
    low = (numbers & 31).astype(F32).astype(BF16)
    every = 32.0 * dot(spread, high) + dot(spread, low)
    place = iota((count, LANES), 0) & (SLOTS - 1)
    columns = []
    for start in first:
        lane = iota((count, LANES), 1) == place + start
        columns.append(jnp.sum(jnp.where(lane, every, 0.0), axis=1, keepdims=True).astype(I32))
    return columns


def one_hot(column, width):
    hit = iota((column.shape[0], width), 1) == column
    return hit.astype(F32).astype(BF16)


def moved_down(x, rows):
    return pltpu.roll(x.reshape(x.shape[0] // 8, 8, x.shape[1]), rows, 1).reshape(x.shape)


def fetch_kernel(numbers, table, out, sent, sems):
    owners = numbers.shape[0]
    rows, width = table.shape
    part = width // 4
    cut = width - part
    hist, cand = number_column(numbers[...], (0, SLOTS))
    step = owners // FETCH_PARTS
    count = step * SLOTS
    last = (iota((count, 1), 0) & (SLOTS - 1)) == SLOTS - 1
    copies = []
    for i in range(FETCH_PARTS):
        mine = slice(i * step, (i + 1) * step)
        block = pl.ds(i * step, step)
        wide = slice(i * count, (i + 1) * count)
        whole = dot(one_hot(hist[wide], rows), table[...])
        sent[mine, :, :width] = whole.astype(BF16).reshape(step, SLOTS, width)
        side = pl.ds(0, width)
        copies += started(
            ((sent.at[block, :, side], out.at[block, :, side]),), sems.at[pl.ds(2 * i, 1)]
        )
        whole = dot(one_hot(cand[wide], rows), table[...])
        ends = whole[:, cut:]
        ends = [moved_down(ends, SLOTS - 1 - s) for s in range(SLOTS - 1)]
        both = jnp.where(last, jnp.concatenate(ends, axis=1), whole[:, :cut])
        sent[mine, :, width:] = both.astype(BF16).reshape(step, SLOTS, cut)
        side = pl.ds(width, cut)
        copies += started(
            ((sent.at[block, :, side], out.at[block, :, side]),), sems.at[pl.ds(2 * i + 1, 1)]
        )
    for copy in copies:
        copy.wait()


def fetch(numbers, table):
    owners = numbers.shape[0]
    rows, width = table.shape
    shape = (owners, SLOTS, 2 * width - width // 4)
    return pl.pallas_call(
        fetch_kernel,
        out_shape=jax.ShapeDtypeStruct(shape, BF16),
        in_specs=[VMEM, VMEM],
        out_specs=HBM,
        scratch_shapes=[pltpu.VMEM(shape, BF16), DMA((2 * FETCH_PARTS,))],
        compiler_params=pltpu.CompilerParams(vmem_limit_bytes=VMEM_BYTES),
        cost_estimate=pl.CostEstimate(
            flops=3 * 10**9, bytes_accessed=3 * 10**6, transcendentals=0
        ),
        name="fetch",
    )(numbers, table)


def picked(dense, column, hot):
    at = column.astype(I32)
    count = dense.shape[0]
    cold = dot(one_hot(at, count), dense)
    return cold + dot(one_hot(at - count, hot.shape[0]), hot[...])


def picked_hist(replies, column, hot):
    owners = replies.shape[0]
    width = hot.shape[1]
    count = owners * SLOTS
    dense = replies[:, :, :width].astype(F32).reshape(count, width).astype(BF16)
    return picked(dense, column, hot)


def picked_cand(replies, column, hot):
    owners = replies.shape[0]
    width = hot.shape[1]
    count = owners * SLOTS
    part = width // 4
    dense = replies[:, :, width:].astype(F32).reshape(count, width - part)
    place = iota((count, 1), 0) & (SLOTS - 1)
    end = moved_down(dense[:, :part], 8 - (SLOTS - 1))
    for s in range(1, SLOTS - 1):
        other = moved_down(dense[:, s * part : (s + 1) * part], 8 - (SLOTS - 1 - s))
        end = jnp.where(place == s, other, end)
    dense = jnp.concatenate([dense, end], axis=1).astype(BF16)
    return picked(dense, column, hot)


def weights(q, k, head_dim):
    half = dot_nt(q, k) * (0.5 / head_dim**0.5)
    return half + half * jnp.tanh(half)


def causal_parts(q, kv, half, at, past, head_dim):
    causal = iota((half, half), 1) <= iota((half, half), 0)

    def masked(w):
        top = jnp.where(causal, w[:half], 0.0)
        if w.shape[0] > half:
            top = jnp.concatenate([top, w[half:]], axis=0)
        return top.astype(BF16)

    first = masked(weights(q[:, at], kv[:half, at], head_dim))
    second = masked(weights(q[half:, at], kv[half:, at], head_dim))
    return dot(first, kv[:half, past]), dot(second, kv[half:, past])


def keys_kernel(
    user, picks, gain, hot, replies, w_in, rows_out, near_out, kv,
    rows, ins, w_v, w_k, w_q, near, sems,
):
    n, width = rows.shape[0] // 2, rows.shape[1]
    hist, cand = pl.ds(0, n), pl.ds(n, n)
    in_v, in_k, in_q = started(
        (
            (w_in.at[:, pl.ds(width, width)], w_v),
            (w_in.at[:, pl.ds(3 * width, width)], w_k),
            (w_in.at[:, pl.ds(2 * width, width)], w_q),
        ),
        sems,
    )
    column = to_column(picks[1:2, :])
    y = picked_cand(replies, column, hot)
    rows[cand, :] = y.astype(BF16)
    ins[cand, :] = norm(y, gain[...]).astype(BF16)
    done = started(
        (
            (rows.at[cand], rows_out.at[cand]),
            (ins.at[cand], rows_out.at[pl.ds(3 * n, n)]),
        ),
        sems.at[pl.ds(4, 2)],
    )
    column = to_column(picks[0:1, :])
    x = picked_hist(replies, column, hot)
    rows[hist, :] = x.astype(BF16)
    inner = norm(x, gain[...]).astype(BF16)
    ins[hist, :] = inner
    done += started(
        (
            (rows.at[hist], rows_out.at[hist]),
            (ins.at[hist], rows_out.at[pl.ds(2 * n, n)]),
        ),
        sems.at[pl.ds(6, 2)],
    )
    in_v.wait()
    kv[:, width:] = silu(dot(inner, w_v[...])).astype(BF16)
    in_k.wait()
    kv[:, :width] = silu(dot(inner, w_k[...])).astype(BF16)
    in_q.wait()

    @pl.when(user[0] == 1)
    def _():
        q = silu(dot(ins[hist, :], w_q[...])).astype(BF16)
        half = n // 2
        head_dim = width // HEADS
        for h in range(HEADS):
            at = slice(h * head_dim, (h + 1) * head_dim)
            past = slice(width + h * head_dim, width + (h + 1) * head_dim)
            first, second = causal_parts(q, kv, half, at, past, head_dim)
            near[:half, at] = first[:half]
            near[half:, at] = first[half:] + second
        (copy,) = started(((near, near_out.at[hist]),), sems.at[pl.ds(8, 1)])
        copy.wait()

    for copy in done:
        copy.wait()


def keys(user, replies, hot, picks, w_in, gain):
    n = picks.shape[1]
    width = hot.shape[1]
    return pl.pallas_call(
        keys_kernel,
        out_shape=(
            jax.ShapeDtypeStruct((SPARE * n, width), BF16),
            jax.ShapeDtypeStruct((SPARE // 2 * n, width), F32),
            jax.ShapeDtypeStruct((n, 2 * width), BF16),
        ),
        in_specs=[SMEM] + [VMEM] * 4 + [HBM],
        out_specs=(HBM, HBM, VMEM),
        scratch_shapes=[
            pltpu.VMEM((2 * n, width), BF16),
            pltpu.VMEM((2 * n, width), BF16),
            pltpu.VMEM((width, width), BF16),
            pltpu.VMEM((width, width), BF16),
            pltpu.VMEM((width, width), BF16),
            pltpu.VMEM((n, width), F32),
            DMA((9,)),
        ],
        compiler_params=pltpu.CompilerParams(vmem_limit_bytes=KEYS_BYTES),
        cost_estimate=pl.CostEstimate(
            flops=3 * 10**9, bytes_accessed=6 * 10**6, transcendentals=10**6
        ),
        name="keys",
    )(user, picks, gain, hot, replies, w_in)


def queries_kernel(rows_in, w_in, qs, ins, w_q, sems):
    n, width = ins.shape[0] // 2, ins.shape[1]
    hist, cand = pl.ds(0, n), pl.ds(n, n)
    in_hist, in_q, in_cand = started(
        (
            (rows_in.at[pl.ds(2 * n, n)], ins.at[hist]),
            (w_in.at[:, pl.ds(2 * width, width)], w_q),
            (rows_in.at[pl.ds(3 * n, n)], ins.at[cand]),
        ),
        sems,
    )
    in_hist.wait()
    in_q.wait()
    qs[hist, :] = silu(dot(ins[hist, :], w_q[...])).astype(BF16)
    in_cand.wait()
    qs[cand, :] = silu(dot(ins[cand, :], w_q[...])).astype(BF16)


def queries(rows, w_in):
    n, width = rows.shape[0] // SPARE, rows.shape[1]
    return pl.pallas_call(
        queries_kernel,
        out_shape=jax.ShapeDtypeStruct((2 * n, width), BF16),
        in_specs=[HBM, HBM],
        out_specs=VMEM,
        scratch_shapes=[
            pltpu.VMEM((2 * n, width), BF16),
            pltpu.VMEM((width, width), BF16),
            DMA((3,)),
        ],
        compiler_params=pltpu.CompilerParams(vmem_limit_bytes=QUERY_BYTES),
        cost_estimate=pl.CostEstimate(
            flops=2 * 10**9, bytes_accessed=4 * 10**6, transcendentals=10**6
        ),
        name="queries",
    )(rows, w_in)


def layer_kernel(
    user, gain, qs, own, other, rows_in, near_in, w_in, w_last, hist_out, cand_out,
    xs, ins, near, w_u, w_out, us, mix, outs, sems,
):
    n, width = own.shape[0], own.shape[1] // 2
    head_dim = width // HEADS
    hist, cand = pl.ds(0, n), pl.ds(n, n)
    both = pl.ds(0, 2 * n)
    arrivals = started(
        (
            (rows_in.at[pl.ds(2 * n, 2 * n)], ins),
            (w_in.at[:, pl.ds(0, width)], w_u),
            (w_last, w_out),
            (rows_in.at[both], xs),
        ),
        sems,
    )
    def gates():
        for arrival in arrivals:
            arrival.wait()
        us[...] = silu(dot(ins[...], w_u[...]))

    half = n // 2

    @pl.when(user[0] == 1)
    def _():
        last = 4 + 2 * FINISH_PARTS
        (copy,) = started(((near_in.at[hist], near),), sems.at[pl.ds(last, 1)])
        for h in range(HEADS):
            if h == HEADS - 1:
                gates()
            at = slice(h * head_dim, (h + 1) * head_dim)
            past = slice(width + h * head_dim, width + (h + 1) * head_dim)
            first = weights(qs[n:, at], own[:, at], head_dim).astype(BF16)
            first = dot(first, own[:, past])
            far = weights(qs[:, at], other[:, at], head_dim).astype(BF16)
            far = dot(far, other[:, past])
            mix[:n, at] = far[:n]
            mix[n:, at] = first + far[n:]
        copy.wait()
        mix[:n, :] += near[...]

    @pl.when(user[0] == 0)
    def _():
        for h in range(HEADS):
            if h == HEADS - 1:
                gates()
            at = slice(h * head_dim, (h + 1) * head_dim)
            past = slice(width + h * head_dim, width + (h + 1) * head_dim)
            first, second = causal_parts(qs, own, half, at, past, head_dim)
            far = weights(qs[n:, at], other[:, at], head_dim).astype(BF16)
            far = dot(far, other[:, past])
            mix[:half, at] = first[:half]
            mix[half:n, at] = first[half:n] + second[: n - half]
            mix[n:, at] = first[n:] + second[n - half :] + far

    done = []
    step = n // FINISH_PARTS
    for i in range(2 * FINISH_PARTS):
        rows = pl.ds(i * step, step)
        out = hist_out if i < FINISH_PARTS else cand_out
        gated = (norm(mix[rows, :], gain[...]) * us[rows, :]).astype(BF16)
        outs[rows, :] = (xs[rows, :].astype(F32) + dot(gated, w_out[...])).astype(BF16)
        place = pl.ds(i % FINISH_PARTS * step, step)
        done += started(((outs.at[rows], out.at[place]),), sems.at[pl.ds(4 + i, 1)])
    for copy in done:
        copy.wait()


def layer(user, rows, near, qs, own, other, gain, w_in, w_out):
    n, width = own.shape[0], own.shape[1] // 2
    shape = jax.ShapeDtypeStruct((n, width), BF16)
    return pl.pallas_call(
        layer_kernel,
        out_shape=(shape, shape),
        in_specs=[SMEM] + [VMEM] * 4 + [HBM] * 4,
        out_specs=(HBM, HBM),
        scratch_shapes=[
            pltpu.VMEM((2 * n, width), BF16),
            pltpu.VMEM((2 * n, width), BF16),
            pltpu.VMEM((n, width), F32),
            pltpu.VMEM((width, width), BF16),
            pltpu.VMEM((width, width), BF16),
            pltpu.VMEM((2 * n, width), F32),
            pltpu.VMEM((2 * n, width), F32),
            pltpu.VMEM((2 * n, width), BF16),
            DMA((5 + 2 * FINISH_PARTS,)),
        ],
        compiler_params=pltpu.CompilerParams(vmem_limit_bytes=LAYER_BYTES),
        cost_estimate=pl.CostEstimate(
            flops=6 * 10**9, bytes_accessed=9 * 10**6, transcendentals=6 * 10**6
        ),
        name="layer",
    )(user, gain, qs, own, other, rows, near, w_in, w_out)


def exchange(array):
    return lax.all_to_all(array, ("req", "cand"), 0, 0, tiled=True)


def per_device(table, hot_table, hot_ids, hist_ids, cand_ids, w_in, w_out, in_gain, attn_gain):
    owners = lax.axis_size("req") * lax.axis_size("cand")
    shift = (table.shape[0] - 1).bit_length()
    asked, picks = ask(hist_ids, cand_ids, hot_ids[None], owners, shift)
    numbers = exchange(asked[:, None, :])[:, 0, :]
    replies = exchange(fetch(numbers, table))
    user = lax.axis_index("user")[None].astype(I32)
    rows, near, own = keys(user, replies, hot_table, picks, w_in[0], in_gain)
    other = lax.ppermute(own, "user", [(0, 1), (1, 0)])
    qs = queries(rows, w_in[0])
    hist_out, cand_out = layer(user, rows, near, qs, own, other, attn_gain, w_in[0], w_out[0])
    return hist_out[None], cand_out[None]


def solution(mesh):
    rows = P(("req", "cand"), None)
    split = P(("req", "cand"), "user")
    in_specs = (rows, P(), P(), split, split, P(), P(), P(), P())
    out_specs = (P(("req", "cand"), "user", None), P(("req", "cand"), "user", None))
    return jax.shard_map(
        per_device, mesh=mesh, in_specs=in_specs, out_specs=out_specs, check_vma=False
    )
```
